512 devices in a mesh: tower: 2 (over x_lo), blk: 128 (over z, x_hi, y), mp: 2 (over core).
Axes of the slice: x: 4 (x_hi: 2, x_lo: 2; x = x_hi * 2 + x_lo), y: 8, z: 8, core: 2. Of those that a mesh axis runs over, the one named last changes fastest.
Arguments:
- tower_inputs: bfloat16 [2, 2048, 2, 18432], P('tower', 'blk', 'mp'), may hold values from -10 to 10
- image_proj: bfloat16 [1536, 1536], P('mp'), may hold values from -4 to 4
- text_proj: bfloat16 [1152, 1536], P('mp'), may hold values from -4 to 4
- text_lengths: int32 [2048], P('blk'), may hold values from 1 to 32
- partner: int32 [2048], P('blk'), may hold values from 0 to 2047, as said below
- log_scale: float32 [1], replicated, may hold values from 2 to 2.6
- bias: float32 [1], replicated, may hold values from -2.5 to -1
Outputs:
- emb_grads: float32 [2, 2048, 1536], P('tower', ('blk', 'mp'))
- loss_sums: float32 [2, 2048], P('tower', ('blk', 'mp'))
The draws below stay inside these ranges and needn't reach their ends.
Inputs may be any that keep to these rules, and one draw needn't show every extreme that they name: `text_lengths`: the number of real tokens of each text; slots past it are padding. Image p is paired with text partner[p]; every text is paired with exactly one image.
All inputs are finite; a program needn't handle non-finite values.
Results may differ from the reference program's by a relative error of at most 0.0015.
Values may be sent and summed in bfloat16 or wider, within the bound.
No kernel may reach another device: no remote copies, remote signals or barrier semaphores. Data moves between devices by JAX's collectives and lax.ppermute only.
A program may use at most 64 MiB of HBM per device.

```python
import jax
import jax.numpy as jnp
from jax import lax

D_IMG = 1536
D_TXT = 1152
EMB = 1536
ROWS = 16
PATCHES = 24
LEN = 32
PAIRS = 2048
SLICE = 18432
N_MP = 2


def pairing(key):
    return jax.random.permutation(jax.random.fold_in(key, 5), PAIRS).astype(jnp.int32)


def projection(key, row_count, gain):
    noise = jax.random.truncated_normal(key, -6.0, 6.0, (row_count, EMB), jnp.float32) * row_count ** (-0.5)
    diagonal = (jnp.arange(row_count)[:, None] == jnp.arange(EMB)[None, :]).astype(jnp.float32)
    return (noise + gain * diagonal).astype(jnp.bfloat16)


def token_block(latent, noise, width):
    parted = latent.reshape(PAIRS, N_MP, 1, width // N_MP) + noise
    parted = jnp.clip(parted, -10.0, 10.0)
    return parted.reshape(PAIRS, N_MP, noise.shape[2] * (width // N_MP))


def draw_partner(key, part):
    return pairing(key)


def draw_image_proj(key, part):
    key = jax.random.fold_in(key, 11)
    return projection(key, D_IMG, 3.0)


def draw_text_proj(key, part):
    key = jax.random.fold_in(key, 12)
    return projection(key, D_TXT, 3.0)


def draw_tower_inputs(key, part):
    order = pairing(key)
    key = jax.random.fold_in(key, 13)
    keys = jax.random.split(key, 8)
    width = max(D_IMG, D_TXT)
    groups = max(PAIRS // 256, 1)
    group_id = jax.random.randint(keys[0], (PAIRS,), 0, groups)
    centers = jax.random.normal(keys[1], (groups, width), jnp.float32)
    common_part = centers[group_id]
    own_part = jax.random.normal(keys[2], (PAIRS, width), jnp.float32)
    text_part = jax.random.normal(keys[3], (PAIRS, width), jnp.float32)
    image_shape = (PAIRS, N_MP, PATCHES, D_IMG // N_MP)
    text_shape = (PAIRS, N_MP, LEN, D_TXT // N_MP)
    latent = 0.6 * common_part + 0.67 * own_part
    image_noise = jax.random.normal(keys[6], image_shape, jnp.float32)
    text_noise = jax.random.normal(keys[7], text_shape, jnp.float32)
    text_latent = jnp.zeros((PAIRS, width), jnp.float32).at[order].set(latent) + 0.3 * text_part
    image_tokens = token_block(latent[:, :D_IMG], image_noise, D_IMG)
    text_tokens = token_block(text_latent[:, :D_TXT], text_noise, D_TXT)
    return jnp.stack([image_tokens, text_tokens]).astype(jnp.bfloat16)


def touch_ends(drawn, key, least, top_value):
    longest = drawn.shape.index(max(drawn.shape))
    spots = []
    for shift in (0, 1):
        where = [jax.random.randint(jax.random.fold_in(key, axis), (), 0, length) for axis, length in enumerate(drawn.shape)]
        where[longest] = (where[longest] + shift) % drawn.shape[longest]
        spots.append(tuple(where))
    return drawn.at[spots[0]].set(least).at[spots[1]].set(top_value)


def setup_inputs(seed: int = 0) -> dict:
    key_list = jax.random.split(jax.random.key(seed), 8)
    return {
        "tower_inputs": draw_tower_inputs(jax.random.fold_in(key_list[7], 71), 0),
        "image_proj": draw_image_proj(jax.random.fold_in(key_list[7], 71), 0),
        "text_proj": draw_text_proj(jax.random.fold_in(key_list[7], 71), 0),
        "text_lengths": touch_ends(jax.random.randint(key_list[3], (PAIRS,), 1, LEN + 1), jax.random.fold_in(key_list[3], 1), 1, LEN).astype(jnp.int32),
        "partner": draw_partner(jax.random.fold_in(key_list[7], 71), 0),
        "log_scale": jnp.clip(jax.random.uniform(key_list[5], (1,), jnp.float32, 2.0, 2.6), 2.0, 2.6),
        "bias": jnp.clip(jax.random.uniform(key_list[6], (1,), jnp.float32, -2.5, -1.0), -2.5, -1.0),
    }


EPS = 1e-06

def image_pool(block_inputs):
    row_count = block_inputs.shape[0]
    parted = block_inputs.astype(jnp.float32).reshape(row_count, N_MP, PATCHES, D_IMG // N_MP)
    summed = lax.optimization_barrier(jnp.sum(parted, axis=2))
    return (summed / PATCHES).reshape(row_count, D_IMG).astype(jnp.bfloat16)

def text_pool(block_inputs, block_lengths):
    row_count = block_inputs.shape[0]
    parted = block_inputs.astype(jnp.float32).reshape(row_count, N_MP, LEN, D_TXT // N_MP)
    keep_mask = (jnp.arange(LEN, dtype=jnp.int32)[None, :] < block_lengths[:, None]).astype(jnp.float32)
    summed = jnp.einsum('rmlf,rl->rmf', parted, keep_mask)
    pooled = summed / block_lengths.astype(jnp.float32)[:, None, None]
    return pooled.reshape(row_count, D_TXT).astype(jnp.bfloat16)

def normalize(embedding):
    inverse = lax.rsqrt(lax.optimization_barrier(jnp.sum(embedding * embedding, axis=1, keepdims=True)) + EPS)
    return (embedding * inverse, inverse)

def one_side(own_low, own_key, other_low, other_key, temper, offset):
    blocks = PAIRS // ROWS

    def block_terms(operands):
        block_low, block_key = operands
        logits = temper * jnp.dot(block_low, other_low.T, preferred_element_type=jnp.float32) + offset
        paired = block_key[:, None] == other_key[None, :]
        losses = jax.nn.softplus(jnp.where(paired, -logits, logits))
        weights = (jax.nn.sigmoid(logits) - paired.astype(jnp.float32)).astype(jnp.bfloat16)
        grad_block = temper * jnp.dot(weights, other_low, preferred_element_type=jnp.float32)
        return (grad_block, lax.optimization_barrier(jnp.sum(losses, axis=1)))
    grads, losses = lax.map(block_terms, (own_low.reshape(blocks, ROWS, EMB), own_key.reshape(blocks, ROWS)))
    return (grads.reshape(PAIRS, EMB), losses.reshape(PAIRS))

def reference(tower_inputs, image_proj, text_proj, text_lengths, partner, log_scale, bias):
    blocks = PAIRS // ROWS
    image_blocks = tower_inputs[0].reshape(blocks, ROWS, N_MP, SLICE)
    text_blocks = tower_inputs[1].reshape(blocks, ROWS, N_MP, SLICE)
    pooled_image = lax.map(image_pool, image_blocks).reshape(PAIRS, D_IMG)
    pooled_text = lax.map(lambda operands: text_pool(operands[0], operands[1]), (text_blocks, text_lengths.reshape(blocks, ROWS))).reshape(PAIRS, D_TXT)
    image_emb = jnp.dot(pooled_image, image_proj, preferred_element_type=jnp.float32)
    text_emb = jnp.dot(pooled_text, text_proj, preferred_element_type=jnp.float32)
    image_unit, image_inverse = normalize(image_emb)
    text_unit, text_inverse = normalize(text_emb)
    image_low = image_unit.astype(jnp.bfloat16)
    text_low = text_unit.astype(jnp.bfloat16)
    temper = jnp.exp(log_scale[0])
    offset = bias[0]
    text_index = jnp.arange(PAIRS, dtype=jnp.int32)
    d_image, image_loss = one_side(image_low, partner, text_low, text_index, temper, offset)
    d_text, text_loss = one_side(text_low, text_index, image_low, partner, temper, offset)
    image_grad = image_inverse * (d_image - image_unit * lax.optimization_barrier(jnp.sum(image_unit * d_image, axis=1, keepdims=True)))
    text_grad = text_inverse * (d_text - text_unit * lax.optimization_barrier(jnp.sum(text_unit * d_text, axis=1, keepdims=True)))
    return (jnp.stack([image_grad, text_grad]), jnp.stack([image_loss, text_loss]))
```

```python
import jax
import jax.numpy as jnp
from jax import lax
from jax.experimental import pallas as pl
from jax.experimental.pallas import tpu as pltpu
from jax.sharding import Mesh
from jax.sharding import PartitionSpec as P

EPS = 1e-06
PIECE = 256
LANES = 128
BASE = 16


def project(pooled, weights, copies, core_ref, keep_ref, send_ref):
    total = None
    for copy, first, last in copies:
        copy.wait()
        piece = jnp.dot(
            pooled[:, first:last], weights[first:last, :], preferred_element_type=jnp.float32
        )
        total = piece if total is None else total + piece
    share = keep_ref.shape[0]
    upper, lower = total[:share], total[share:]
    first_core = core_ref[0] == 0
    keep_ref[...] = jnp.where(first_core, upper, lower)
    send_ref[...] = jnp.where(first_core, lower, upper)


def fetch(slices_hbm, weights_hbm, slices, weights, sems):
    depth = weights_hbm.shape[0]
    first_copy = pltpu.make_async_copy(slices_hbm, slices, sems.at[0])
    first_copy.start()
    copies = []
    for place, first in enumerate(range(0, depth, PIECE)):
        last = min(first + PIECE, depth)
        copy = pltpu.make_async_copy(
            weights_hbm.at[first:last], weights.at[first:last], sems.at[1 + place]
        )
        copy.start()
        copies.append((copy, first, min(first + PIECE, weights.shape[0])))
    return first_copy, copies


def image_kernel(core_ref, slices_hbm, weights_hbm, keep_ref, send_ref, slices, weights, sems):
    first_copy, copies = fetch(slices_hbm, weights_hbm, slices, weights, sems)
    width = weights_hbm.shape[0]
    patch_count = slices.shape[1] // width
    first_copy.wait()
    summed = slices[:, :width].astype(jnp.float32)
    for patch in range(1, patch_count):
        summed += slices[:, patch * width : (patch + 1) * width].astype(jnp.float32)
    pooled = (summed / patch_count).astype(jnp.bfloat16)
    project(pooled, weights, copies, core_ref, keep_ref, send_ref)


def text_kernel(
    core_ref, lengths_ref, slices_hbm, weights_hbm, keep_ref, send_ref, slices, weights, sems
):
    first_copy, copies = fetch(slices_hbm, weights_hbm, slices, weights, sems)
    width = weights_hbm.shape[0]
    row_count = slices.shape[0]
    slot_count = slices.shape[1] // width
    padded = weights.shape[0]
    if padded > width:
        weights[width:, :] = jnp.zeros((padded - width, weights.shape[1]), jnp.bfloat16)
    shape = (row_count, 2 * width)
    row = lax.broadcasted_iota(jnp.int32, shape, 0)
    lengths = jnp.zeros(shape, jnp.int32)
    for index in range(row_count):
        lengths = jnp.where(row == index, lengths_ref[index], lengths)
    second = (lax.broadcasted_iota(jnp.int32, shape, 1) >= width).astype(jnp.int32)
    left = lengths - second
    first_copy.wait()
    summed = jnp.zeros(shape, jnp.float32)
    for slot in range(0, slot_count, 2):
        piece = slices[:, slot * width : (slot + 2) * width].astype(jnp.float32)
        summed += jnp.where(slot < left, piece, 0.0)
    summed = summed + pltpu.roll(summed, width, 1)
    pooled = (summed / lengths.astype(jnp.float32)).astype(jnp.bfloat16)
    project(pooled, weights, copies, core_ref, keep_ref, send_ref)


def pooled_partial(kernel, scalars, slices, weights):
    row_count = slices.shape[0]
    depth, width = weights.shape
    padded = -(-depth // LANES) * LANES
    pieces = -(-depth // PIECE)
    any_space = pl.BlockSpec(memory_space=pl.ANY)
    half = jax.ShapeDtypeStruct((row_count // 2, width), jnp.float32)
    return pl.pallas_call(
        kernel,
        out_shape=(half, half),
        in_specs=[pl.BlockSpec(memory_space=pltpu.SMEM)] * len(scalars) + [any_space] * 2,
        out_specs=(pl.BlockSpec(memory_space=pltpu.VMEM),) * 2,
        scratch_shapes=[
            pltpu.VMEM(slices.shape, jnp.bfloat16),
            pltpu.VMEM((padded, width), jnp.bfloat16),
            pltpu.SemaphoreType.DMA((1 + pieces,)),
        ],
        compiler_params=pltpu.CompilerParams(vmem_limit_bytes=32 * 2**20),
    )(*scalars, slices, weights)


def swap_gather(block, axis, after):
    members = lax.axis_size(axis)
    half = members // 2
    size = block.shape[0]

    def brought(value, across):
        return lax.ppermute(value, axis, [(index, index ^ across) for index in range(members)])

    pair = jnp.concatenate([block, brought(block, half)], axis=0)
    pair, _ = lax.optimization_barrier((pair, after))
    held = jnp.concatenate([pair] + [brought(pair, across) for across in range(1, half)], axis=0)
    place = lax.broadcasted_iota(jnp.int32, (members * size, members * size), 0)
    slot = lax.broadcasted_iota(jnp.int32, (members * size, members * size), 1)
    number = slot // size
    came_from = lax.axis_index(axis) ^ (number // 2 + (number % 2) * half)
    moves = (place // size == came_from) & (place % size == slot % size)
    ordered = jnp.dot(moves.astype(held.dtype), held, preferred_element_type=jnp.float32)
    return ordered.astype(held.dtype)


def shards(tower_inputs, image_proj, text_proj, text_lengths, partner, log_scale, bias):
    slices = tower_inputs[0, :, 0, :]
    row_count = slices.shape[0]
    tower = lax.axis_index("tower")
    core = lax.axis_index("mp")
    n_mp = lax.axis_size("mp")
    n_y = lax.axis_size("y")
    n_x = lax.axis_size("x")
    n_z = lax.axis_size("z")
    share = row_count // n_mp
    width = image_proj.shape[1]

    core_index = core.astype(jnp.int32).reshape(1)
    kept, sent = lax.cond(
        tower == 0,
        lambda: pooled_partial(image_kernel, (core_index,), slices, image_proj),
        lambda: pooled_partial(text_kernel, (core_index, text_lengths), slices, text_proj),
    )
    embedding = kept + lax.ppermute(sent, "mp", [(0, 1), (1, 0)])
    inverse = lax.rsqrt(jnp.sum(embedding * embedding, axis=1, keepdims=True) + EPS)
    unit = embedding * inverse
    unit_low = unit.astype(jnp.bfloat16)

    key = lax.dynamic_slice_in_dim(partner, core * share, share, 0)
    key_high = (key // BASE).astype(jnp.bfloat16)[:, None]
    key_low = (key % BASE).astype(jnp.bfloat16)[:, None]
    column = lax.broadcasted_iota(jnp.int32, (share, LANES), 1)
    key_block = jnp.where(column == 0, key_high, jnp.where(column == 1, key_low, 0))
    own = jnp.concatenate([unit_low, key_block], axis=1)

    near = lax.ppermute(own, "tower", [(0, 1), (1, 0)])
    across = lax.ppermute(own, ("tower", "x"), [(0, 3), (3, 0), (1, 2), (2, 1)])
    other = jnp.concatenate([near, across], axis=0)
    copies = jnp.broadcast_to(other[None], (n_y,) + other.shape)
    own_all = swap_gather(own, "z", other[:1, :LANES])
    other_mine = lax.all_to_all(copies, "y", 0, 0, tiled=True)
    other_mine = other_mine.reshape(n_y * n_x * share, width + LANES)
    other_theirs = lax.ppermute(other_mine, "mp", [(0, 1), (1, 0)])

    def sent_key(gathered):
        pair = gathered[:, width : width + 2].astype(jnp.int32)
        return pair[:, 0] * BASE + pair[:, 1]

    z = lax.axis_index("z")
    y = lax.axis_index("y")
    x = lax.axis_index("x")

    def pair_at(z_at, x_at, y_at):
        return ((z_at * n_x + x_at) * n_y + y_at) * row_count

    own_slot = lax.iota(jnp.int32, n_z * share)
    own_place = pair_at(own_slot // share, x, y) + core * share + own_slot % share
    other_slot = lax.iota(jnp.int32, n_y * n_x * share)
    other_x = x ^ (other_slot // share % n_x)
    other_base = pair_at(z, other_x, other_slot // (n_x * share)) + other_slot % share
    own_key = jnp.where(tower == 0, sent_key(own_all), own_place)
    temper = jnp.exp(log_scale[0])
    own_low = own_all[:, :width]

    def score(others, other_core):
        other_place = other_base + other_core * share
        other_key = jnp.where(tower == 0, other_place, sent_key(others))
        other_low = others[:, :width]
        logits = (
            temper
            * lax.dot_general(
                own_low, other_low, (((1,), (1,)), ((), ())), preferred_element_type=jnp.float32
            )
            + bias[0]
        )
        paired = own_key[:, None] == other_key[None, :]
        losses = jax.nn.softplus(jnp.where(paired, -logits, logits))
        weights = (jax.nn.sigmoid(logits) - paired.astype(jnp.float32)).astype(jnp.bfloat16)
        grad = jnp.dot(weights, other_low, preferred_element_type=jnp.float32)
        return grad, jnp.sum(losses, axis=1, keepdims=True)

    grad_mine, loss_mine = score(other_mine, core)
    grad_theirs, loss_theirs = score(other_theirs, 1 - core)
    grad_part = grad_mine + grad_theirs
    loss_part = loss_mine + loss_theirs

    loss_high = lax.reduce_precision(loss_part, 5, 10)
    loss_rest = loss_part - loss_high
    lane = lax.broadcasted_iota(jnp.int32, (n_z * share, LANES), 1)
    loss_block = jnp.where(lane == 0, loss_high, loss_rest).astype(jnp.float16)
    sums = jnp.concatenate([grad_part.astype(jnp.float16), loss_block], axis=1)
    sums = lax.all_to_all(sums.reshape(n_z, share, width + LANES), "z", 0, 0, tiled=True)
    total = jnp.sum(sums.astype(jnp.float32), axis=0)
    grad_sum = temper * total[:, :width]
    loss_sum = total[:, width] + total[:, width + 1]

    along = jnp.sum(unit * grad_sum, axis=1, keepdims=True)
    gradient = inverse * (grad_sum - unit * along)
    return (gradient[None], loss_sum[None])


def solution(mesh):
    n_tower, n_blk, n_mp = (mesh.shape[name] for name in ("tower", "blk", "mp"))
    n_z, n_x = 8, 2
    grid = Mesh(
        mesh.devices.reshape(n_tower, n_z, n_x, n_blk // (n_z * n_x), n_mp),
        ("tower", "z", "x", "y", "mp"),
    )
    blk = ("z", "x", "y")
    placed = (
        P("tower", blk, "mp", None),
        P("mp", None),
        P("mp", None),
        P(blk),
        P(blk),
        P(),
        P(),
    )
    return jax.shard_map(
        shards,
        mesh=grid,
        in_specs=placed,
        out_specs=(P("tower", blk + ("mp",), None), P("tower", blk + ("mp",))),
        check_vma=False,
    )
```

```python
import jax
import jax.numpy as jnp
from jax import lax
from jax.experimental import pallas as pl
from jax.experimental.pallas import tpu as pltpu
from jax.sharding import Mesh
from jax.sharding import PartitionSpec as P

EPS = 1e-06
PIECE = 256
LANES = 128
BASE = 16


def project(pooled, weights, copies, core_ref, keep_ref, send_ref):
    total = None
    for copy, first, last in copies:
        copy.wait()
        piece = jnp.dot(
            pooled[:, first:last], weights[first:last, :], preferred_element_type=jnp.float32
        )
        total = piece if total is None else total + piece
    share = keep_ref.shape[0]
    upper, lower = total[:share], total[share:]
    first_core = core_ref[0] == 0
    keep_ref[...] = jnp.where(first_core, upper, lower)
    send_ref[...] = jnp.where(first_core, lower, upper)


def fetch(slices_hbm, weights_hbm, slices, weights, sems):
    depth = weights_hbm.shape[0]
    first_copy = pltpu.make_async_copy(slices_hbm, slices, sems.at[0])
    first_copy.start()
    copies = []
    for place, first in enumerate(range(0, depth, PIECE)):
        last = min(first + PIECE, depth)
        copy = pltpu.make_async_copy(
            weights_hbm.at[first:last], weights.at[first:last], sems.at[1 + place]
        )
        copy.start()
        copies.append((copy, first, min(first + PIECE, weights.shape[0])))
    return first_copy, copies


def image_kernel(core_ref, slices_hbm, weights_hbm, keep_ref, send_ref, slices, weights, sems):
    first_copy, copies = fetch(slices_hbm, weights_hbm, slices, weights, sems)
    width = weights_hbm.shape[0]
    patch_count = slices.shape[1] // width
    first_copy.wait()
    summed = slices[:, :width].astype(jnp.float32)
    for patch in range(1, patch_count):
        summed += slices[:, patch * width : (patch + 1) * width].astype(jnp.float32)
    pooled = (summed / patch_count).astype(jnp.bfloat16)
    project(pooled, weights, copies, core_ref, keep_ref, send_ref)


def text_kernel(
    core_ref, lengths_hbm, slices_hbm, weights_hbm, keep_ref, send_ref, slices, weights, sems, lengths_ref
):
    lengths_copy = pltpu.make_async_copy(lengths_hbm, lengths_ref, sems.at[sems.shape[0] - 1])
    lengths_copy.start()
    first_copy, copies = fetch(slices_hbm, weights_hbm, slices, weights, sems)
    width = weights_hbm.shape[0]
    row_count = slices.shape[0]
    slot_count = slices.shape[1] // width
    padded = weights.shape[0]
    if padded > width:
        weights[width:, :] = jnp.zeros((padded - width, weights.shape[1]), jnp.bfloat16)
    shape = (row_count, 2 * width)
    row = lax.broadcasted_iota(jnp.int32, shape, 0)
    lengths = jnp.zeros(shape, jnp.int32)
    lengths_copy.wait()
    for index in range(row_count):
        lengths = jnp.where(row == index, lengths_ref[index], lengths)
    second = (lax.broadcasted_iota(jnp.int32, shape, 1) >= width).astype(jnp.int32)
    left = lengths - second
    first_copy.wait()
    summed = jnp.zeros(shape, jnp.float32)
    for slot in range(0, slot_count, 2):
        piece = slices[:, slot * width : (slot + 2) * width].astype(jnp.float32)
        summed += jnp.where(slot < left, piece, 0.0)
    summed = summed + pltpu.roll(summed, width, 1)
    pooled = (summed / lengths.astype(jnp.float32)).astype(jnp.bfloat16)
    project(pooled, weights, copies, core_ref, keep_ref, send_ref)


def pooled_partial(kernel, core_index, slices, weights, lengths=None):
    row_count = slices.shape[0]
    depth, width = weights.shape
    padded = -(-depth // LANES) * LANES
    pieces = -(-depth // PIECE)
    any_space = pl.BlockSpec(memory_space=pl.ANY)
    half = jax.ShapeDtypeStruct((row_count // 2, width), jnp.float32)
    given = (slices, weights) if lengths is None else (lengths, slices, weights)
    scratch = [
        pltpu.VMEM(slices.shape, jnp.bfloat16),
        pltpu.VMEM((padded, width), jnp.bfloat16),
        pltpu.SemaphoreType.DMA((2 + pieces,)),
    ]
    if lengths is not None:
        scratch.append(pltpu.SMEM(lengths.shape, jnp.int32))
    return pl.pallas_call(
        kernel,
        out_shape=(half, half),
        in_specs=[pl.BlockSpec(memory_space=pltpu.SMEM)] + [any_space] * len(given),
        out_specs=(pl.BlockSpec(memory_space=pltpu.VMEM),) * 2,
        scratch_shapes=scratch,
        compiler_params=pltpu.CompilerParams(vmem_limit_bytes=32 * 2**20),
    )(core_index, *given)


def mirrored(blocks, axis):
    members = lax.axis_size(axis)
    cores = lax.axis_size("mp")
    groups = [
        [at * cores + core for at in (range(members) if core == 0 else reversed(range(members)))]
        for core in range(cores)
    ]
    return lax.all_to_all(blocks, (axis, "mp"), 0, 0, axis_index_groups=groups, tiled=True)


def swap_gather(block, axis, after):
    members = lax.axis_size(axis)
    half = members // 2
    size = block.shape[0]

    def brought(value, across):
        return lax.ppermute(value, axis, [(index, index ^ across) for index in range(members)])

    pair = jnp.concatenate([block, brought(block, half)], axis=0)
    pair, _ = lax.optimization_barrier((pair, after))
    held = jnp.concatenate([pair] + [brought(pair, across) for across in range(1, half)], axis=0)
    place = lax.broadcasted_iota(jnp.int32, (members * size, members * size), 0)
    slot = lax.broadcasted_iota(jnp.int32, (members * size, members * size), 1)
    number = slot // size
    came_from = lax.axis_index(axis) ^ (number // 2 + (number % 2) * half)
    member = jnp.where(lax.axis_index("mp") == 0, place // size, members - 1 - place // size)
    moves = (member == came_from) & (place % size == slot % size)
    ordered = jnp.dot(moves.astype(held.dtype), held, preferred_element_type=jnp.float32)
    return ordered.astype(held.dtype)


def shards(tower_inputs, image_proj, text_proj, text_lengths, partner, log_scale, bias):
    slices = tower_inputs[0, :, 0, :]
    row_count = slices.shape[0]
    tower = lax.axis_index("tower")
    core = lax.axis_index("mp")
    n_mp = lax.axis_size("mp")
    n_y = lax.axis_size("y")
    n_x = lax.axis_size("x")
    n_z = lax.axis_size("z")
    share = row_count // n_mp
    width = image_proj.shape[1]

    core_index = core.astype(jnp.int32).reshape(1)
    kept, sent = lax.cond(
        tower == 0,
        lambda: pooled_partial(image_kernel, core_index, slices, image_proj),
        lambda: pooled_partial(text_kernel, core_index, slices, text_proj, text_lengths),
    )
    embedding = kept + lax.ppermute(sent, "mp", [(0, 1), (1, 0)])
    inverse = lax.rsqrt(jnp.sum(embedding * embedding, axis=1, keepdims=True) + EPS)
    unit = embedding * inverse
    unit_low = unit.astype(jnp.bfloat16)

    key = lax.dynamic_slice_in_dim(partner, core * share, share, 0)
    key_high = (key // BASE).astype(jnp.bfloat16)[:, None]
    key_low = (key % BASE).astype(jnp.bfloat16)[:, None]
    column = lax.broadcasted_iota(jnp.int32, (share, LANES), 1)
    key_block = jnp.where(column == 0, key_high, jnp.where(column == 1, key_low, 0))
    own = jnp.concatenate([unit_low, key_block], axis=1)

    near = lax.ppermute(own, "tower", [(0, 1), (1, 0)])
    across = lax.ppermute(own, ("tower", "x"), [(0, 3), (3, 0), (1, 2), (2, 1)])
    other = jnp.concatenate([near, across], axis=0)
    copies = jnp.broadcast_to(other[None], (n_y,) + other.shape)
    own_all = swap_gather(own, "z", other[:1, :LANES])
    other_mine = mirrored(copies, "y")
    other_mine = other_mine.reshape(n_y * n_x * share, width + LANES)
    other_theirs = lax.ppermute(other_mine, "mp", [(0, 1), (1, 0)])

    def sent_key(gathered):
        pair = gathered[:, width : width + 2].astype(jnp.int32)
        return pair[:, 0] * BASE + pair[:, 1]

    z = lax.axis_index("z")
    y = lax.axis_index("y")
    x = lax.axis_index("x")

    def pair_at(z_at, x_at, y_at):
        return ((z_at * n_x + x_at) * n_y + y_at) * row_count

    own_slot = lax.iota(jnp.int32, n_z * share)
    own_z = jnp.where(core == 0, own_slot // share, n_z - 1 - own_slot // share)
    own_place = pair_at(own_z, x, y) + core * share + own_slot % share
    other_slot = lax.iota(jnp.int32, n_y * n_x * share)
    other_x = x ^ (other_slot // share % n_x)
    other_y = other_slot // (n_x * share)
    other_reversed = n_y - 1 - other_y
    own_key = jnp.where(tower == 0, sent_key(own_all), own_place)
    temper = jnp.exp(log_scale[0])
    own_low = own_all[:, :width]

    def score(others, other_core):
        other_at = jnp.where(other_core == 0, other_y, other_reversed)
        other_place = pair_at(z, other_x, other_at) + other_core * share + other_slot % share
        other_key = jnp.where(tower == 0, other_place, sent_key(others))
        other_low = others[:, :width]
        logits = (
            temper
            * lax.dot_general(
                own_low, other_low, (((1,), (1,)), ((), ())), preferred_element_type=jnp.float32
            )
            + bias[0]
        )
        paired = own_key[:, None] == other_key[None, :]
        losses = jax.nn.softplus(jnp.where(paired, -logits, logits))
        weights = (jax.nn.sigmoid(logits) - paired.astype(jnp.float32)).astype(jnp.bfloat16)
        grad = jnp.dot(weights, other_low, preferred_element_type=jnp.float32)
        return grad, jnp.sum(losses, axis=1, keepdims=True)

    grad_mine, loss_mine = score(other_mine, core)
    grad_theirs, loss_theirs = score(other_theirs, 1 - core)
    grad_part = grad_mine + grad_theirs
    loss_part = loss_mine + loss_theirs

    loss_high = lax.reduce_precision(loss_part, 5, 10)
    loss_rest = loss_part - loss_high
    lane = lax.broadcasted_iota(jnp.int32, (n_z * share, LANES), 1)
    loss_block = jnp.where(lane == 0, loss_high, loss_rest).astype(jnp.float16)
    sums = jnp.concatenate([grad_part.astype(jnp.float16), loss_block], axis=1)
    sums = mirrored(sums.reshape(n_z, share, width + LANES), "z")
    total = jnp.sum(sums.astype(jnp.float32), axis=0)
    grad_sum = temper * total[:, :width]
    loss_sum = total[:, width] + total[:, width + 1]

    along = jnp.sum(unit * grad_sum, axis=1, keepdims=True)
    gradient = inverse * (grad_sum - unit * along)
    return (gradient[None], loss_sum[None])


def solution(mesh):
    n_tower, n_blk, n_mp = (mesh.shape[name] for name in ("tower", "blk", "mp"))
    n_z, n_x = 8, 2
    grid = Mesh(
        mesh.devices.reshape(n_tower, n_z, n_x, n_blk // (n_z * n_x), n_mp),
        ("tower", "z", "x", "y", "mp"),
    )
    blk = ("z", "x", "y")
    placed = (
        P("tower", blk, "mp", None),
        P("mp", None),
        P("mp", None),
        P(blk),
        P(blk),
        P(),
        P(),
    )
    return jax.shard_map(
        shards,
        mesh=grid,
        in_specs=placed,
        out_specs=(P("tower", blk + ("mp",), None), P("tower", blk + ("mp",))),
        check_vma=False,
    )
```

```python
import jax
import jax.numpy as jnp
from jax import lax
from jax.experimental import pallas as pl
from jax.experimental.pallas import tpu as pltpu
from jax.sharding import Mesh
from jax.sharding import PartitionSpec as P

EPS = 1e-06
PIECE = 256
LANES = 128
BASE = 16


def project(pooled, weights, copies, core_ref, keep_ref, send_ref):
    total = None
    for copy, first, last in copies:
        copy.wait()
        piece = jnp.dot(
            pooled[:, first:last], weights[first:last, :], preferred_element_type=jnp.float32
        )
        total = piece if total is None else total + piece
    share = keep_ref.shape[0]
    upper, lower = total[:share], total[share:]
    first_core = core_ref[0] == 0
    keep_ref[...] = jnp.where(first_core, upper, lower)
    send_ref[...] = jnp.where(first_core, lower, upper)


def fetch(slices_hbm, weights_hbm, slices, weights, sems):
    depth = weights_hbm.shape[0]
    first_copy = pltpu.make_async_copy(slices_hbm, slices, sems.at[0])
    first_copy.start()
    copies = []
    for place, first in enumerate(range(0, depth, PIECE)):
        last = min(first + PIECE, depth)
        copy = pltpu.make_async_copy(
            weights_hbm.at[first:last], weights.at[first:last], sems.at[1 + place]
        )
        copy.start()
        copies.append((copy, first, min(first + PIECE, weights.shape[0])))
    return first_copy, copies


def image_kernel(core_ref, slices_hbm, weights_hbm, keep_ref, send_ref, slices, weights, sems):
    first_copy, copies = fetch(slices_hbm, weights_hbm, slices, weights, sems)
    width = weights_hbm.shape[0]
    patch_count = slices.shape[1] // width
    first_copy.wait()
    summed = slices[:, :width].astype(jnp.float32)
    for patch in range(1, patch_count):
        summed += slices[:, patch * width : (patch + 1) * width].astype(jnp.float32)
    pooled = (summed / patch_count).astype(jnp.bfloat16)
    project(pooled, weights, copies, core_ref, keep_ref, send_ref)


def text_kernel(
    core_ref, lengths_hbm, slices_hbm, weights_hbm, keep_ref, send_ref, slices, weights, sems, lengths_ref
):
    lengths_copy = pltpu.make_async_copy(lengths_hbm, lengths_ref, sems.at[sems.shape[0] - 1])
    lengths_copy.start()
    first_copy, copies = fetch(slices_hbm, weights_hbm, slices, weights, sems)
    width = weights_hbm.shape[0]
    row_count = slices.shape[0]
    slot_count = slices.shape[1] // width
    padded = weights.shape[0]
    if padded > width:
        weights[width:, :] = jnp.zeros((padded - width, weights.shape[1]), jnp.bfloat16)
    shape = (row_count, 2 * width)
    row = lax.broadcasted_iota(jnp.int32, shape, 0)
    lengths = jnp.zeros(shape, jnp.int32)
    lengths_copy.wait()
    for index in range(row_count):
        lengths = jnp.where(row == index, lengths_ref[index], lengths)
    second = (lax.broadcasted_iota(jnp.int32, shape, 1) >= width).astype(jnp.int32)
    left = lengths - second
    first_copy.wait()
    summed = jnp.zeros(shape, jnp.float32)
    for slot in range(0, slot_count, 2):
        piece = slices[:, slot * width : (slot + 2) * width].astype(jnp.float32)
        summed += jnp.where(slot < left, piece, 0.0)
    summed = summed + pltpu.roll(summed, width, 1)
    pooled = (summed / lengths.astype(jnp.float32)).astype(jnp.bfloat16)
    project(pooled, weights, copies, core_ref, keep_ref, send_ref)


def pooled_partial(kernel, core_index, slices, weights, lengths=None):
    row_count = slices.shape[0]
    depth, width = weights.shape
    padded = -(-depth // LANES) * LANES
    pieces = -(-depth // PIECE)
    any_space = pl.BlockSpec(memory_space=pl.ANY)
    half = jax.ShapeDtypeStruct((row_count // 2, width), jnp.float32)
    given = (slices, weights) if lengths is None else (lengths, slices, weights)
    scratch = [
        pltpu.VMEM(slices.shape, jnp.bfloat16),
        pltpu.VMEM((padded, width), jnp.bfloat16),
        pltpu.SemaphoreType.DMA((2 + pieces,)),
    ]
    if lengths is not None:
        scratch.append(pltpu.SMEM(lengths.shape, jnp.int32))
    return pl.pallas_call(
        kernel,
        out_shape=(half, half),
        in_specs=[pl.BlockSpec(memory_space=pltpu.SMEM)] + [any_space] * len(given),
        out_specs=(pl.BlockSpec(memory_space=pltpu.VMEM),) * 2,
        scratch_shapes=scratch,
        compiler_params=pltpu.CompilerParams(vmem_limit_bytes=32 * 2**20),
    )(core_index, *given)


def mirrored(blocks, axis):
    members = lax.axis_size(axis)
    cores = lax.axis_size("mp")
    groups = [
        [at * cores + core for at in (range(members) if core == 0 else reversed(range(members)))]
        for core in range(cores)
    ]
    return lax.all_to_all(blocks, (axis, "mp"), 0, 0, axis_index_groups=groups, tiled=True)


def swap_gather(block, axis, after):
    members = lax.axis_size(axis)
    half = members // 2
    size = block.shape[0]

    def brought(value, across):
        return lax.ppermute(value, axis, [(index, index ^ across) for index in range(members)])

    pair = jnp.concatenate([block, brought(block, half)], axis=0)
    pair, _ = lax.optimization_barrier((pair, after))
    held = jnp.concatenate([pair] + [brought(pair, across) for across in range(1, half)], axis=0)
    place = lax.broadcasted_iota(jnp.int32, (members * size, members * size), 0)
    slot = lax.broadcasted_iota(jnp.int32, (members * size, members * size), 1)
    number = slot // size
    came_from = lax.axis_index(axis) ^ (number // 2 + (number % 2) * half)
    member = jnp.where(lax.axis_index("mp") == 0, place // size, members - 1 - place // size)
    moves = (member == came_from) & (place % size == slot % size)
    ordered = jnp.dot(moves.astype(held.dtype), held, preferred_element_type=jnp.float32)
    return ordered.astype(held.dtype)


def final_kernel(scale_ref, total_ref, embedding_ref, grads_hbm, losses_hbm, grads, losses, sems):
    share, width = embedding_ref.shape
    loss = total_ref[:, width : width + 1] + total_ref[:, width + 1 : width + 2]
    row = lax.broadcasted_iota(jnp.int32, (share, LANES), 0)
    column = lax.broadcasted_iota(jnp.int32, (share, LANES), 1)
    diagonal = jnp.where(row == column, jnp.broadcast_to(loss, (share, LANES)), 0.0)
    losses[...] = jnp.sum(diagonal, axis=0, keepdims=True)[:, :share]
    losses_copy = pltpu.make_async_copy(losses, losses_hbm, sems.at[0])
    losses_copy.start()
    embedding = embedding_ref[...]
    inverse = lax.rsqrt(jnp.sum(embedding * embedding, axis=1, keepdims=True) + EPS)
    unit = embedding * inverse
    grad_sum = jnp.exp(jnp.full((1, LANES), scale_ref[0], jnp.float32))[:, :1] * total_ref[:, :width]
    along = jnp.sum(unit * grad_sum, axis=1, keepdims=True)
    grads[0] = inverse * (grad_sum - unit * along)
    grads_copy = pltpu.make_async_copy(grads, grads_hbm, sems.at[1])
    grads_copy.start()
    losses_copy.wait()
    grads_copy.wait()


def shards(tower_inputs, image_proj, text_proj, text_lengths, partner, log_scale, bias):
    slices = tower_inputs[0, :, 0, :]
    row_count = slices.shape[0]
    tower = lax.axis_index("tower")
    core = lax.axis_index("mp")
    n_mp = lax.axis_size("mp")
    n_y = lax.axis_size("y")
    n_x = lax.axis_size("x")
    n_z = lax.axis_size("z")
    share = row_count // n_mp
    width = image_proj.shape[1]

    core_index = core.astype(jnp.int32).reshape(1)
    kept, sent = lax.cond(
        tower == 0,
        lambda: pooled_partial(image_kernel, core_index, slices, image_proj),
        lambda: pooled_partial(text_kernel, core_index, slices, text_proj, text_lengths),
    )
    embedding = kept + lax.ppermute(sent, "mp", [(0, 1), (1, 0)])
    inverse = lax.rsqrt(jnp.sum(embedding * embedding, axis=1, keepdims=True) + EPS)
    unit = embedding * inverse
    unit_low = unit.astype(jnp.bfloat16)

    key = lax.dynamic_slice_in_dim(partner, core * share, share, 0)
    key_high = (key // BASE).astype(jnp.bfloat16)[:, None]
    key_low = (key % BASE).astype(jnp.bfloat16)[:, None]
    column = lax.broadcasted_iota(jnp.int32, (share, LANES), 1)
    key_block = jnp.where(column == 0, key_high, jnp.where(column == 1, key_low, 0))
    own = jnp.concatenate([unit_low, key_block], axis=1)

    near = lax.ppermute(own, "tower", [(0, 1), (1, 0)])
    across = lax.ppermute(own, ("tower", "x"), [(0, 3), (3, 0), (1, 2), (2, 1)])
    other = jnp.concatenate([near, across], axis=0)
    copies = jnp.broadcast_to(other[None], (n_y,) + other.shape)
    own_all = swap_gather(own, "z", other[:1, :LANES])
    other_mine = mirrored(copies, "y")
    other_mine = other_mine.reshape(n_y * n_x * share, width + LANES)
    other_theirs = lax.ppermute(other_mine, "mp", [(0, 1), (1, 0)])

    def sent_key(gathered):
        pair = gathered[:, width : width + 2].astype(jnp.int32)
        return pair[:, 0] * BASE + pair[:, 1]

    z = lax.axis_index("z")
    y = lax.axis_index("y")
    x = lax.axis_index("x")

    def pair_at(z_at, x_at, y_at):
        return ((z_at * n_x + x_at) * n_y + y_at) * row_count

    own_slot = lax.iota(jnp.int32, n_z * share)
    own_z = jnp.where(core == 0, own_slot // share, n_z - 1 - own_slot // share)
    own_place = pair_at(own_z, x, y) + core * share + own_slot % share
    other_slot = lax.iota(jnp.int32, n_y * n_x * share)
    other_x = x ^ (other_slot // share % n_x)
    other_y = other_slot // (n_x * share)
    other_reversed = n_y - 1 - other_y
    own_key = jnp.where(tower == 0, sent_key(own_all), own_place)
    temper = jnp.exp(log_scale[0])
    own_low = own_all[:, :width]

    def score(others, other_core):
        other_at = jnp.where(other_core == 0, other_y, other_reversed)
        other_place = pair_at(z, other_x, other_at) + other_core * share + other_slot % share
        other_key = jnp.where(tower == 0, other_place, sent_key(others))
        other_low = others[:, :width]
        logits = (
            temper
            * lax.dot_general(
                own_low, other_low, (((1,), (1,)), ((), ())), preferred_element_type=jnp.float32
            )
            + bias[0]
        )
        paired = own_key[:, None] == other_key[None, :]
        losses = jax.nn.softplus(jnp.where(paired, -logits, logits))
        weights = (jax.nn.sigmoid(logits) - paired.astype(jnp.float32)).astype(jnp.bfloat16)
        grad = jnp.dot(weights, other_low, preferred_element_type=jnp.float32)
        return grad, jnp.sum(losses, axis=1, keepdims=True)

    grad_mine, loss_mine = score(other_mine, core)
    grad_theirs, loss_theirs = score(other_theirs, 1 - core)
    grad_part = grad_mine + grad_theirs
    loss_part = loss_mine + loss_theirs

    loss_high = lax.reduce_precision(loss_part, 5, 10)
    loss_rest = loss_part - loss_high
    lane = lax.broadcasted_iota(jnp.int32, (n_z * share, LANES), 1)
    loss_block = jnp.where(lane == 0, loss_high, loss_rest).astype(jnp.float16)
    sums = jnp.concatenate([grad_part.astype(jnp.float16), loss_block], axis=1)
    sums = mirrored(sums.reshape(n_z, share, width + LANES), "z")
    total = jnp.sum(sums.astype(jnp.float32), axis=0)
    vmem = pl.BlockSpec(memory_space=pltpu.VMEM)
    any_space = pl.BlockSpec(memory_space=pl.ANY)
    return pl.pallas_call(
        final_kernel,
        out_shape=(
            jax.ShapeDtypeStruct((1, share, width), jnp.float32),
            jax.ShapeDtypeStruct((1, share), jnp.float32),
        ),
        in_specs=[pl.BlockSpec(memory_space=pltpu.SMEM), vmem, vmem],
        out_specs=(any_space, any_space),
        scratch_shapes=[
            pltpu.VMEM((1, share, width), jnp.float32),
            pltpu.VMEM((1, share), jnp.float32),
            pltpu.SemaphoreType.DMA((2,)),
        ],
        compiler_params=pltpu.CompilerParams(vmem_limit_bytes=8 * 2**20),
    )(log_scale, total, embedding)


def solution(mesh):
    n_tower, n_blk, n_mp = (mesh.shape[name] for name in ("tower", "blk", "mp"))
    n_z, n_x = 8, 2
    grid = Mesh(
        mesh.devices.reshape(n_tower, n_z, n_x, n_blk // (n_z * n_x), n_mp),
        ("tower", "z", "x", "y", "mp"),
    )
    blk = ("z", "x", "y")
    placed = (
        P("tower", blk, "mp", None),
        P("mp", None),
        P("mp", None),
        P(blk),
        P(blk),
        P(),
        P(),
    )
    return jax.shard_map(
        shards,
        mesh=grid,
        in_specs=placed,
        out_specs=(P("tower", blk + ("mp",), None), P("tower", blk + ("mp",))),
        check_vma=False,
    )
```

```python
import jax
import jax.numpy as jnp
from jax import lax
from jax.experimental import pallas as pl
from jax.experimental.pallas import tpu as pltpu
from jax.sharding import Mesh
from jax.sharding import PartitionSpec as P

EPS = 1e-06
PIECE = 256
LANES = 128
HIGH, LOW = 64, 32
SUMS = 3


def project(pooled, weights, copies, core_ref, keep_ref, send_ref):
    total = None
    for copy, first, last in copies:
        copy.wait()
        piece = jnp.dot(
            pooled[:, first:last], weights[first:last, :], preferred_element_type=jnp.float32
        )
        total = piece if total is None else total + piece
    share = keep_ref.shape[0]
    upper, lower = total[:share], total[share:]
    first_core = core_ref[0] == 0
    keep_ref[...] = jnp.where(first_core, upper, lower)
    send_ref[...] = jnp.where(first_core, lower, upper)


def fetch(slices_hbm, weights_hbm, slices, weights, sems):
    depth = weights_hbm.shape[0]
    first_copy = pltpu.make_async_copy(slices_hbm, slices, sems.at[0])
    first_copy.start()
    copies = []
    for place, first in enumerate(range(0, depth, PIECE)):
        last = min(first + PIECE, depth)
        copy = pltpu.make_async_copy(
            weights_hbm.at[first:last], weights.at[first:last], sems.at[1 + place]
        )
        copy.start()
        copies.append((copy, first, min(first + PIECE, weights.shape[0])))
    return first_copy, copies


def image_kernel(core_ref, slices_hbm, weights_hbm, keep_ref, send_ref, slices, weights, sems):
    first_copy, copies = fetch(slices_hbm, weights_hbm, slices, weights, sems)
    width = weights_hbm.shape[0]
    patch_count = slices.shape[1] // width
    first_copy.wait()
    summed = slices[:, :width].astype(jnp.float32)
    for patch in range(1, patch_count):
        summed += slices[:, patch * width : (patch + 1) * width].astype(jnp.float32)
    pooled = (summed / patch_count).astype(jnp.bfloat16)
    project(pooled, weights, copies, core_ref, keep_ref, send_ref)


def text_kernel(
    core_ref, lengths_hbm, slices_hbm, weights_hbm, keep_ref, send_ref, slices, weights, sems, lengths_ref
):
    lengths_copy = pltpu.make_async_copy(lengths_hbm, lengths_ref, sems.at[sems.shape[0] - 1])
    lengths_copy.start()
    first_copy, copies = fetch(slices_hbm, weights_hbm, slices, weights, sems)
    width = weights_hbm.shape[0]
    row_count = slices.shape[0]
    slot_count = slices.shape[1] // width
    padded = weights.shape[0]
    if padded > width:
        weights[width:, :] = jnp.zeros((padded - width, weights.shape[1]), jnp.bfloat16)
    shape = (row_count, 2 * width)
    row = lax.broadcasted_iota(jnp.int32, shape, 0)
    lengths = jnp.zeros(shape, jnp.int32)
    lengths_copy.wait()
    for index in range(row_count):
        lengths = jnp.where(row == index, lengths_ref[index], lengths)
    second = (lax.broadcasted_iota(jnp.int32, shape, 1) >= width).astype(jnp.int32)
    left = lengths - second
    first_copy.wait()
    summed = jnp.zeros(shape, jnp.float32)
    for slot in range(0, slot_count, 2):
        piece = slices[:, slot * width : (slot + 2) * width].astype(jnp.float32)
        summed += jnp.where(slot < left, piece, 0.0)
    summed = summed + pltpu.roll(summed, width, 1)
    pooled = (summed / lengths.astype(jnp.float32)).astype(jnp.bfloat16)
    project(pooled, weights, copies, core_ref, keep_ref, send_ref)


def pooled_partial(kernel, core_index, slices, weights, lengths=None):
    row_count = slices.shape[0]
    depth, width = weights.shape
    padded = -(-depth // LANES) * LANES
    pieces = -(-depth // PIECE)
    any_space = pl.BlockSpec(memory_space=pl.ANY)
    half = jax.ShapeDtypeStruct((row_count // 2, width), jnp.float32)
    given = (slices, weights) if lengths is None else (lengths, slices, weights)
    scratch = [
        pltpu.VMEM(slices.shape, jnp.bfloat16),
        pltpu.VMEM((padded, width), jnp.bfloat16),
        pltpu.SemaphoreType.DMA((2 + pieces,)),
    ]
    if lengths is not None:
        scratch.append(pltpu.SMEM(lengths.shape, jnp.int32))
    return pl.pallas_call(
        kernel,
        out_shape=(half, half),
        in_specs=[pl.BlockSpec(memory_space=pltpu.SMEM)] + [any_space] * len(given),
        out_specs=(pl.BlockSpec(memory_space=pltpu.VMEM),) * 2,
        scratch_shapes=scratch,
        compiler_params=pltpu.CompilerParams(vmem_limit_bytes=32 * 2**20),
    )(core_index, *given)


def staggered(blocks, axis):
    members = lax.axis_size(axis)
    cores = lax.axis_size("mp")
    groups = [
        [(at ^ (core * (members // 2))) * cores + core for at in range(members)]
        for core in range(cores)
    ]
    return lax.all_to_all(blocks, (axis, "mp"), 0, 0, axis_index_groups=groups, tiled=True)


def swap_gather(block, axis):
    members = lax.axis_size(axis)
    half = members // 2

    def brought(value, across):
        return lax.ppermute(value, axis, [(index, index ^ across) for index in range(members)])

    pair = jnp.concatenate([block, brought(block, half)], axis=0)
    wide = pair.astype(jnp.float32)
    passed = jnp.sum(wide, axis=0, keepdims=True)
    for _ in range(SUMS - 1):
        passed = jnp.sum(wide * passed, axis=0, keepdims=True)
    pair = pair + (passed * 0).astype(pair.dtype)
    return jnp.concatenate([pair] + [brought(pair, across) for across in range(1, half)], axis=0)


def in_order(held, axis, size, last):
    members = lax.axis_size(axis)
    place = lax.broadcasted_iota(jnp.int32, (members * size, members * size), 0)
    slot = lax.broadcasted_iota(jnp.int32, (members * size, members * size), 1)
    number = slot // size
    came_from = lax.axis_index(axis) ^ (number // 2 + (number % 2) * (members // 2))
    member = (place // size) ^ (lax.axis_index("mp") * (members // 2))
    moves = (member == came_from) & (place % size == slot % size)
    moves = moves.astype(held.dtype) + last[: members * size, : members * size] * 0
    ordered = jnp.dot(moves, held, preferred_element_type=jnp.float32)
    return ordered.astype(held.dtype)


def final_kernel(scale_ref, total_ref, embedding_ref, grads_hbm, losses_hbm, grads, losses, sems):
    share, width = embedding_ref.shape
    loss = total_ref[:, width : width + 1] + total_ref[:, width + 1 : width + 2]
    row = lax.broadcasted_iota(jnp.int32, (share, LANES), 0)
    column = lax.broadcasted_iota(jnp.int32, (share, LANES), 1)
    diagonal = jnp.where(row == column, jnp.broadcast_to(loss, (share, LANES)), 0.0)
    losses[...] = jnp.sum(diagonal, axis=0, keepdims=True)[:, :share]
    losses_copy = pltpu.make_async_copy(losses, losses_hbm, sems.at[0])
    losses_copy.start()
    embedding = embedding_ref[...]
    inverse = lax.rsqrt(jnp.sum(embedding * embedding, axis=1, keepdims=True) + EPS)
    unit = embedding * inverse
    grad_sum = jnp.exp(jnp.full((1, LANES), scale_ref[0], jnp.float32))[:, :1] * total_ref[:, :width]
    along = jnp.sum(unit * grad_sum, axis=1, keepdims=True)
    grads[0] = inverse * (grad_sum - unit * along)
    grads_copy = pltpu.make_async_copy(grads, grads_hbm, sems.at[1])
    grads_copy.start()
    losses_copy.wait()
    grads_copy.wait()


def shards(tower_inputs, image_proj, text_proj, text_lengths, partner, log_scale, bias):
    slices = tower_inputs[0, :, 0, :]
    row_count = slices.shape[0]
    tower = lax.axis_index("tower")
    core = lax.axis_index("mp")
    n_mp = lax.axis_size("mp")
    n_y = lax.axis_size("y")
    n_x = lax.axis_size("x")
    n_z = lax.axis_size("z")
    share = row_count // n_mp
    width = image_proj.shape[1]

    def pair_at(z_at, x_at, y_at):
        return ((z_at * n_x + x_at) * n_y + y_at) * row_count

    core_index = core.astype(jnp.int32).reshape(1)
    kept, sent = lax.cond(
        tower == 0,
        lambda: pooled_partial(image_kernel, core_index, slices, image_proj),
        lambda: pooled_partial(text_kernel, core_index, slices, text_proj, text_lengths),
    )
    embedding = kept + lax.ppermute(sent, "mp", [(0, 1), (1, 0)])
    inverse = lax.rsqrt(jnp.sum(embedding * embedding, axis=1, keepdims=True) + EPS)
    unit = embedding * inverse
    unit_low = unit.astype(jnp.bfloat16)

    first = pair_at(lax.axis_index("z"), lax.axis_index("x"), lax.axis_index("y")) + core * share
    partners = lax.dynamic_slice_in_dim(partner, core * share, share, 0)
    key = jnp.where(tower == 0, partners, first + lax.iota(jnp.int32, share))[:, None]
    column = lax.broadcasted_iota(jnp.int32, (share, LANES), 1)
    coded = (column == key // LOW) | (column == HIGH + key % LOW)
    key_block = coded.astype(jnp.bfloat16)
    own = jnp.concatenate([unit_low, key_block], axis=1)

    near = lax.ppermute(own, "tower", [(0, 1), (1, 0)])
    across = lax.ppermute(own, ("tower", "x"), [(0, 3), (3, 0), (1, 2), (2, 1)])
    other = jnp.concatenate([near, across], axis=0)
    copies = jnp.broadcast_to(other[None], (n_y,) + other.shape)
    held = swap_gather(own, "z")
    other_mine = staggered(copies, "y")
    other_mine = other_mine.reshape(n_y * n_x * share, width + LANES)
    other_theirs = lax.ppermute(other_mine, "mp", [(0, 1), (1, 0)])
    own_all = in_order(held, "z", share, other_mine)

    temper = jnp.exp(log_scale[0])
    own_low = own_all[:, :width]

    def products(rows, columns):
        return lax.dot_general(
            rows, columns, (((1,), (1,)), ((), ())), preferred_element_type=jnp.float32
        )

    def score(others):
        other_low = others[:, :width]
        logits = temper * products(own_low, other_low) + bias[0]
        paired = products(own_all[:, width:], others[:, width:]) > 1.5
        losses = jax.nn.softplus(jnp.where(paired, -logits, logits))
        weights = (jax.nn.sigmoid(logits) - paired.astype(jnp.float32)).astype(jnp.bfloat16)
        grad = jnp.dot(weights, other_low, preferred_element_type=jnp.float32)
        return grad, jnp.sum(losses, axis=1, keepdims=True)

    grad_mine, loss_mine = score(other_mine)
    grad_theirs, loss_theirs = score(other_theirs)
    grad_part = grad_mine + grad_theirs
    loss_part = loss_mine + loss_theirs

    loss_high = lax.reduce_precision(loss_part, 5, 10)
    loss_rest = loss_part - loss_high
    lane = lax.broadcasted_iota(jnp.int32, (n_z * share, LANES), 1)
    loss_block = jnp.where(lane == 0, loss_high, loss_rest).astype(jnp.float16)
    sums = jnp.concatenate([grad_part.astype(jnp.float16), loss_block], axis=1)
    sums = staggered(sums.reshape(n_z, share, width + LANES), "z")
    total = jnp.sum(sums.astype(jnp.float32), axis=0)
    vmem = pl.BlockSpec(memory_space=pltpu.VMEM)
    any_space = pl.BlockSpec(memory_space=pl.ANY)
    return pl.pallas_call(
        final_kernel,
        out_shape=(
            jax.ShapeDtypeStruct((1, share, width), jnp.float32),
            jax.ShapeDtypeStruct((1, share), jnp.float32),
        ),
        in_specs=[pl.BlockSpec(memory_space=pltpu.SMEM), vmem, vmem],
        out_specs=(any_space, any_space),
        scratch_shapes=[
            pltpu.VMEM((1, share, width), jnp.float32),
            pltpu.VMEM((1, share), jnp.float32),
            pltpu.SemaphoreType.DMA((2,)),
        ],
        compiler_params=pltpu.CompilerParams(vmem_limit_bytes=8 * 2**20),
    )(log_scale, total, embedding)


def solution(mesh):
    n_tower, n_blk, n_mp = (mesh.shape[name] for name in ("tower", "blk", "mp"))
    n_z, n_x = 8, 2
    grid = Mesh(
        mesh.devices.reshape(n_tower, n_z, n_x, n_blk // (n_z * n_x), n_mp),
        ("tower", "z", "x", "y", "mp"),
    )
    blk = ("z", "x", "y")
    placed = (
        P("tower", blk, "mp", None),
        P("mp", None),
        P("mp", None),
        P(blk),
        P(blk),
        P(),
        P(),
    )
    return jax.shard_map(
        shards,
        mesh=grid,
        in_specs=placed,
        out_specs=(P("tower", blk + ("mp",), None), P("tower", blk + ("mp",))),
        check_vma=False,
    )
```

```python
import jax
import jax.numpy as jnp
from jax import lax
from jax.experimental import pallas as pl
from jax.experimental.pallas import tpu as pltpu
from jax.sharding import Mesh
from jax.sharding import PartitionSpec as P

EPS = 1e-06
PIECE = 256
QUARTERS = 4
LANES = 128
HIGH, LOW = 64, 32
SUMS = 3


def project(pooled, weights, copies, core_ref, keep_ref, send_ref):
    total = None
    depth = weights.shape[0]
    for first in range(0, depth, PIECE):
        last = min(first + PIECE, depth)
        for copy, start in copies:
            if first <= start < last:
                copy.wait()
        piece = jnp.dot(
            pooled[:, first:last], weights[first:last, :], preferred_element_type=jnp.float32
        )
        total = piece if total is None else total + piece
    share = keep_ref.shape[0]
    upper, lower = total[:share], total[share:]
    first_core = core_ref[0] == 0
    keep_ref[...] = jnp.where(first_core, upper, lower)
    send_ref[...] = jnp.where(first_core, lower, upper)


def fetch(slices_hbm, weights_hbm, slices, weights, sems):
    depth = weights_hbm.shape[0]
    quarter = slices.shape[1] // QUARTERS
    quarters = []
    for place in range(QUARTERS):
        columns = pl.ds(place * quarter, quarter)
        quarters.append(
            pltpu.make_async_copy(slices_hbm.at[:, columns], slices.at[:, columns], sems.at[place])
        )
        quarters[-1].start()
    copies = []
    for place, first in enumerate(range(0, depth, LANES)):
        rows = pl.ds(first, min(LANES, depth - first))
        copy = pltpu.make_async_copy(
            weights_hbm.at[rows], weights.at[rows], sems.at[QUARTERS + place]
        )
        copy.start()
        copies.append((copy, first))
    return quarters, copies


def image_kernel(core_ref, slices_hbm, weights_hbm, keep_ref, send_ref, slices, weights, sems):
    quarters, copies = fetch(slices_hbm, weights_hbm, slices, weights, sems)
    width = weights_hbm.shape[0]
    patch_count = slices.shape[1] // width
    summed = jnp.zeros((slices.shape[0], width), jnp.float32)
    for patch in range(patch_count):
        if patch % (patch_count // QUARTERS) == 0:
            quarters[patch // (patch_count // QUARTERS)].wait()
        summed += slices[:, patch * width : (patch + 1) * width].astype(jnp.float32)
    pooled = (summed / patch_count).astype(jnp.bfloat16)
    project(pooled, weights, copies, core_ref, keep_ref, send_ref)


def text_kernel(
    core_ref, lengths_hbm, slices_hbm, weights_hbm, keep_ref, send_ref, slices, weights, sems, lengths_ref
):
    lengths_copy = pltpu.make_async_copy(lengths_hbm, lengths_ref, sems.at[sems.shape[0] - 1])
    lengths_copy.start()
    quarters, copies = fetch(slices_hbm, weights_hbm, slices, weights, sems)
    width = weights_hbm.shape[0]
    row_count = slices.shape[0]
    slot_count = slices.shape[1] // width
    padded = weights.shape[0]
    if padded > width:
        weights[width:, :] = jnp.zeros((padded - width, weights.shape[1]), jnp.bfloat16)
    shape = (row_count, 2 * width)
    row = lax.broadcasted_iota(jnp.int32, shape, 0)
    lengths = jnp.zeros(shape, jnp.int32)
    lengths_copy.wait()
    for index in range(row_count):
        lengths = jnp.where(row == index, lengths_ref[index], lengths)
    second = (lax.broadcasted_iota(jnp.int32, shape, 1) >= width).astype(jnp.int32)
    left = lengths - second
    summed = jnp.zeros(shape, jnp.float32)
    for slot in range(0, slot_count, 2):
        if slot % (slot_count // QUARTERS) == 0:
            quarters[slot // (slot_count // QUARTERS)].wait()
        piece = slices[:, slot * width : (slot + 2) * width].astype(jnp.float32)
        summed += jnp.where(slot < left, piece, 0.0)
    summed = summed + pltpu.roll(summed, width, 1)
    pooled = (summed / lengths.astype(jnp.float32)).astype(jnp.bfloat16)
    project(pooled, weights, copies, core_ref, keep_ref, send_ref)


def pooled_partial(kernel, core_index, slices, weights, lengths=None):
    row_count = slices.shape[0]
    depth, width = weights.shape
    padded = -(-depth // LANES) * LANES
    any_space = pl.BlockSpec(memory_space=pl.ANY)
    half = jax.ShapeDtypeStruct((row_count // 2, width), jnp.float32)
    given = (slices, weights) if lengths is None else (lengths, slices, weights)
    scratch = [
        pltpu.VMEM(slices.shape, jnp.bfloat16),
        pltpu.VMEM((padded, width), jnp.bfloat16),
        pltpu.SemaphoreType.DMA((QUARTERS + padded // LANES + 1,)),
    ]
    if lengths is not None:
        scratch.append(pltpu.SMEM(lengths.shape, jnp.int32))
    return pl.pallas_call(
        kernel,
        out_shape=(half, half),
        in_specs=[pl.BlockSpec(memory_space=pltpu.SMEM)] + [any_space] * len(given),
        out_specs=(pl.BlockSpec(memory_space=pltpu.VMEM),) * 2,
        scratch_shapes=scratch,
        compiler_params=pltpu.CompilerParams(vmem_limit_bytes=32 * 2**20),
    )(core_index, *given)


def staggered(blocks, axis):
    members = lax.axis_size(axis)
    cores = lax.axis_size("mp")
    groups = [
        [(at ^ (core * (members // 2))) * cores + core for at in range(members)]
        for core in range(cores)
    ]
    return lax.all_to_all(blocks, (axis, "mp"), 0, 0, axis_index_groups=groups, tiled=True)


def swap_gather(block, axis):
    members = lax.axis_size(axis)
    half = members // 2

    def brought(value, across):
        return lax.ppermute(value, axis, [(index, index ^ across) for index in range(members)])

    pair = jnp.concatenate([block, brought(block, half)], axis=0)
    wide = pair.astype(jnp.float32)
    passed = jnp.sum(wide, axis=0, keepdims=True)
    for _ in range(SUMS - 1):
        passed = jnp.sum(wide * passed, axis=0, keepdims=True)
    pair = pair + (passed * 0).astype(pair.dtype)
    return jnp.concatenate([pair] + [brought(pair, across) for across in range(1, half)], axis=0)


def in_order(held, axis, size, last):
    members = lax.axis_size(axis)
    place = lax.broadcasted_iota(jnp.int32, (members * size, members * size), 0)
    slot = lax.broadcasted_iota(jnp.int32, (members * size, members * size), 1)
    number = slot // size
    came_from = lax.axis_index(axis) ^ (number // 2 + (number % 2) * (members // 2))
    member = (place // size) ^ (lax.axis_index("mp") * (members // 2))
    moves = (member == came_from) & (place % size == slot % size)
    moves = moves.astype(held.dtype) + last[: members * size, : members * size] * 0
    ordered = jnp.dot(moves, held, preferred_element_type=jnp.float32)
    return ordered.astype(held.dtype)


def final_kernel(scale_ref, total_ref, embedding_ref, grads_hbm, losses_hbm, grads, losses, sems):
    share, width = embedding_ref.shape
    loss = total_ref[:, width : width + 1] + total_ref[:, width + 1 : width + 2]
    row = lax.broadcasted_iota(jnp.int32, (share, LANES), 0)
    column = lax.broadcasted_iota(jnp.int32, (share, LANES), 1)
    diagonal = jnp.where(row == column, jnp.broadcast_to(loss, (share, LANES)), 0.0)
    losses[...] = jnp.sum(diagonal, axis=0, keepdims=True)[:, :share]
    losses_copy = pltpu.make_async_copy(losses, losses_hbm, sems.at[0])
    losses_copy.start()
    embedding = embedding_ref[...]
    inverse = lax.rsqrt(jnp.sum(embedding * embedding, axis=1, keepdims=True) + EPS)
    unit = embedding * inverse
    grad_sum = jnp.exp(jnp.full((1, LANES), scale_ref[0], jnp.float32))[:, :1] * total_ref[:, :width]
    along = jnp.sum(unit * grad_sum, axis=1, keepdims=True)
    grads[0] = inverse * (grad_sum - unit * along)
    grads_copy = pltpu.make_async_copy(grads, grads_hbm, sems.at[1])
    grads_copy.start()
    losses_copy.wait()
    grads_copy.wait()


def shards(tower_inputs, image_proj, text_proj, text_lengths, partner, log_scale, bias):
    slices = tower_inputs[0, :, 0, :]
    row_count = slices.shape[0]
    tower = lax.axis_index("tower")
    core = lax.axis_index("mp")
    n_mp = lax.axis_size("mp")
    n_y = lax.axis_size("y")
    n_x = lax.axis_size("x")
    n_z = lax.axis_size("z")
    share = row_count // n_mp
    width = image_proj.shape[1]

    def pair_at(z_at, x_at, y_at):
        return ((z_at * n_x + x_at) * n_y + y_at) * row_count

    core_index = core.astype(jnp.int32).reshape(1)
    kept, sent = lax.cond(
        tower == 0,
        lambda: pooled_partial(image_kernel, core_index, slices, image_proj),
        lambda: pooled_partial(text_kernel, core_index, slices, text_proj, text_lengths),
    )
    embedding = kept + lax.ppermute(sent, "mp", [(0, 1), (1, 0)])
    inverse = lax.rsqrt(jnp.sum(embedding * embedding, axis=1, keepdims=True) + EPS)
    unit = embedding * inverse
    unit_low = unit.astype(jnp.bfloat16)

    first = pair_at(lax.axis_index("z"), lax.axis_index("x"), lax.axis_index("y")) + core * share
    partners = lax.dynamic_slice_in_dim(partner, core * share, share, 0)
    key = jnp.where(tower == 0, partners, first + lax.iota(jnp.int32, share))[:, None]
    column = lax.broadcasted_iota(jnp.int32, (share, LANES), 1)
    coded = (column == key // LOW) | (column == HIGH + key % LOW)
    key_block = coded.astype(jnp.bfloat16)
    own = jnp.concatenate([unit_low, key_block], axis=1)

    near = lax.ppermute(own, "tower", [(0, 1), (1, 0)])
    across = lax.ppermute(own, ("tower", "x"), [(0, 3), (3, 0), (1, 2), (2, 1)])
    other = jnp.concatenate([near, across], axis=0)
    copies = jnp.broadcast_to(other[None], (n_y,) + other.shape)
    held = swap_gather(own, "z")
    other_mine = staggered(copies, "y")
    other_mine = other_mine.reshape(n_y * n_x * share, width + LANES)
    other_theirs = lax.ppermute(other_mine, "mp", [(0, 1), (1, 0)])
    own_all = in_order(held, "z", share, other_mine)

    temper = jnp.exp(log_scale[0])
    own_low = own_all[:, :width]

    def products(rows, columns):
        return lax.dot_general(
            rows, columns, (((1,), (1,)), ((), ())), preferred_element_type=jnp.float32
        )

    def score(others):
        other_low = others[:, :width]
        logits = temper * products(own_low, other_low) + bias[0]
        paired = products(own_all[:, width:], others[:, width:]) > 1.5
        losses = jax.nn.softplus(jnp.where(paired, -logits, logits))
        weights = (jax.nn.sigmoid(logits) - paired.astype(jnp.float32)).astype(jnp.bfloat16)
        grad = jnp.dot(weights, other_low, preferred_element_type=jnp.float32)
        return grad, jnp.sum(losses, axis=1, keepdims=True)

    grad_mine, loss_mine = score(other_mine)
    grad_theirs, loss_theirs = score(other_theirs)
    grad_part = grad_mine + grad_theirs
    loss_part = loss_mine + loss_theirs

    loss_high = lax.reduce_precision(loss_part, 5, 10)
    loss_rest = loss_part - loss_high
    lane = lax.broadcasted_iota(jnp.int32, (n_z * share, LANES), 1)
    loss_block = jnp.where(lane == 0, loss_high, loss_rest).astype(jnp.float16)
    sums = jnp.concatenate([grad_part.astype(jnp.float16), loss_block], axis=1)
    sums = staggered(sums.reshape(n_z, share, width + LANES), "z")
    total = jnp.sum(sums.astype(jnp.float32), axis=0)
    vmem = pl.BlockSpec(memory_space=pltpu.VMEM)
    any_space = pl.BlockSpec(memory_space=pl.ANY)
    return pl.pallas_call(
        final_kernel,
        out_shape=(
            jax.ShapeDtypeStruct((1, share, width), jnp.float32),
            jax.ShapeDtypeStruct((1, share), jnp.float32),
        ),
        in_specs=[pl.BlockSpec(memory_space=pltpu.SMEM), vmem, vmem],
        out_specs=(any_space, any_space),
        scratch_shapes=[
            pltpu.VMEM((1, share, width), jnp.float32),
            pltpu.VMEM((1, share), jnp.float32),
            pltpu.SemaphoreType.DMA((2,)),
        ],
        compiler_params=pltpu.CompilerParams(vmem_limit_bytes=8 * 2**20),
    )(log_scale, total, embedding)


def solution(mesh):
    n_tower, n_blk, n_mp = (mesh.shape[name] for name in ("tower", "blk", "mp"))
    n_z, n_x = 8, 2
    grid = Mesh(
        mesh.devices.reshape(n_tower, n_z, n_x, n_blk // (n_z * n_x), n_mp),
        ("tower", "z", "x", "y", "mp"),
    )
    blk = ("z", "x", "y")
    placed = (
        P("tower", blk, "mp", None),
        P("mp", None),
        P("mp", None),
        P(blk),
        P(blk),
        P(),
        P(),
    )
    return jax.shard_map(
        shards,
        mesh=grid,
        in_specs=placed,
        out_specs=(P("tower", blk + ("mp",), None), P("tower", blk + ("mp",))),
        check_vma=False,
    )
```

```python
import jax
import jax.numpy as jnp
from jax import lax
from jax.experimental import pallas as pl
from jax.experimental.pallas import tpu as pltpu
from jax.sharding import Mesh
from jax.sharding import PartitionSpec as P

EPS = 1e-06
PIECE = 256
LANES = 128
HIGH, LOW = 64, 32
SUMS = 3
FIRST_Z = (4, 6)


def project(pooled, weights, copies, core_ref, keep_ref, send_ref):
    total = None
    for copy, first, last in copies:
        copy.wait()
        piece = jnp.dot(
            pooled[:, first:last], weights[first:last, :], preferred_element_type=jnp.float32
        )
        total = piece if total is None else total + piece
    share = keep_ref.shape[0]
    upper, lower = total[:share], total[share:]
    first_core = core_ref[0] == 0
    keep_ref[...] = jnp.where(first_core, upper, lower)
    send_ref[...] = jnp.where(first_core, lower, upper)


def fetch(slices_hbm, weights_hbm, slices, weights, sems):
    depth = weights_hbm.shape[0]
    first_copy = pltpu.make_async_copy(slices_hbm, slices, sems.at[0])
    first_copy.start()
    copies = []
    for place, first in enumerate(range(0, depth, PIECE)):
        last = min(first + PIECE, depth)
        copy = pltpu.make_async_copy(
            weights_hbm.at[first:last], weights.at[first:last], sems.at[1 + place]
        )
        copy.start()
        copies.append((copy, first, min(first + PIECE, weights.shape[0])))
    return first_copy, copies


def image_kernel(core_ref, slices_hbm, weights_hbm, keep_ref, send_ref, slices, weights, sems):
    first_copy, copies = fetch(slices_hbm, weights_hbm, slices, weights, sems)
    width = weights_hbm.shape[0]
    patch_count = slices.shape[1] // width
    first_copy.wait()
    summed = slices[:, :width].astype(jnp.float32)
    for patch in range(1, patch_count):
        summed += slices[:, patch * width : (patch + 1) * width].astype(jnp.float32)
    pooled = (summed / patch_count).astype(jnp.bfloat16)
    project(pooled, weights, copies, core_ref, keep_ref, send_ref)


def text_kernel(
    core_ref, lengths_hbm, slices_hbm, weights_hbm, keep_ref, send_ref, slices, weights, sems, lengths_ref
):
    lengths_copy = pltpu.make_async_copy(lengths_hbm, lengths_ref, sems.at[sems.shape[0] - 1])
    lengths_copy.start()
    first_copy, copies = fetch(slices_hbm, weights_hbm, slices, weights, sems)
    width = weights_hbm.shape[0]
    row_count = slices.shape[0]
    slot_count = slices.shape[1] // width
    padded = weights.shape[0]
    if padded > width:
        weights[width:, :] = jnp.zeros((padded - width, weights.shape[1]), jnp.bfloat16)
    shape = (row_count, 2 * width)
    row = lax.broadcasted_iota(jnp.int32, shape, 0)
    lengths = jnp.zeros(shape, jnp.int32)
    lengths_copy.wait()
    for index in range(row_count):
        lengths = jnp.where(row == index, lengths_ref[index], lengths)
    second = (lax.broadcasted_iota(jnp.int32, shape, 1) >= width).astype(jnp.int32)
    left = lengths - second
    first_copy.wait()
    summed = jnp.zeros(shape, jnp.float32)
    for slot in range(0, slot_count, 2):
        piece = slices[:, slot * width : (slot + 2) * width].astype(jnp.float32)
        summed += jnp.where(slot < left, piece, 0.0)
    summed = summed + pltpu.roll(summed, width, 1)
    pooled = (summed / lengths.astype(jnp.float32)).astype(jnp.bfloat16)
    project(pooled, weights, copies, core_ref, keep_ref, send_ref)


def pooled_partial(kernel, core_index, slices, weights, lengths=None):
    row_count = slices.shape[0]
    depth, width = weights.shape
    padded = -(-depth // LANES) * LANES
    pieces = -(-depth // PIECE)
    any_space = pl.BlockSpec(memory_space=pl.ANY)
    half = jax.ShapeDtypeStruct((row_count // 2, width), jnp.float32)
    given = (slices, weights) if lengths is None else (lengths, slices, weights)
    scratch = [
        pltpu.VMEM(slices.shape, jnp.bfloat16),
        pltpu.VMEM((padded, width), jnp.bfloat16),
        pltpu.SemaphoreType.DMA((2 + pieces,)),
    ]
    if lengths is not None:
        scratch.append(pltpu.SMEM(lengths.shape, jnp.int32))
    return pl.pallas_call(
        kernel,
        out_shape=(half, half),
        in_specs=[pl.BlockSpec(memory_space=pltpu.SMEM)] + [any_space] * len(given),
        out_specs=(pl.BlockSpec(memory_space=pltpu.VMEM),) * 2,
        scratch_shapes=scratch,
        compiler_params=pltpu.CompilerParams(vmem_limit_bytes=32 * 2**20),
    )(core_index, *given)


def staggered(blocks, axis, firsts):
    members = lax.axis_size(axis)
    cores = lax.axis_size("mp")
    groups = [
        [(at + firsts[core]) % members * cores + core for at in range(members)]
        for core in range(cores)
    ]
    return lax.all_to_all(blocks, (axis, "mp"), 0, 0, axis_index_groups=groups, tiled=True)


def swap_gather(block, axis):
    members = lax.axis_size(axis)
    half = members // 2

    def brought(value, across):
        return lax.ppermute(value, axis, [(index, index ^ across) for index in range(members)])

    pair = jnp.concatenate([block, brought(block, half)], axis=0)
    wide = pair.astype(jnp.float32)
    passed = jnp.sum(wide, axis=0, keepdims=True)
    for _ in range(SUMS - 1):
        passed = jnp.sum(wide * passed, axis=0, keepdims=True)
    pair = pair + (passed * 0).astype(pair.dtype)
    return jnp.concatenate([pair] + [brought(pair, across) for across in range(1, half)], axis=0)


def in_order(held, axis, size, firsts, last):
    members = lax.axis_size(axis)
    place = lax.broadcasted_iota(jnp.int32, (members * size, members * size), 0)
    slot = lax.broadcasted_iota(jnp.int32, (members * size, members * size), 1)
    number = slot // size
    came_from = lax.axis_index(axis) ^ (number // 2 + (number % 2) * (members // 2))
    first = jnp.where(lax.axis_index("mp") == 0, firsts[0], firsts[1])
    member = (place // size + first) % members
    moves = (member == came_from) & (place % size == slot % size)
    moves = moves.astype(held.dtype) + last[: members * size, : members * size] * 0
    ordered = jnp.dot(moves, held, preferred_element_type=jnp.float32)
    return ordered.astype(held.dtype)


def final_kernel(scale_ref, total_ref, embedding_ref, grads_hbm, losses_hbm, grads, losses, sems):
    share, width = embedding_ref.shape
    loss = total_ref[:, width : width + 1] + total_ref[:, width + 1 : width + 2]
    row = lax.broadcasted_iota(jnp.int32, (share, LANES), 0)
    column = lax.broadcasted_iota(jnp.int32, (share, LANES), 1)
    diagonal = jnp.where(row == column, jnp.broadcast_to(loss, (share, LANES)), 0.0)
    losses[...] = jnp.sum(diagonal, axis=0, keepdims=True)[:, :share]
    losses_copy = pltpu.make_async_copy(losses, losses_hbm, sems.at[0])
    losses_copy.start()
    embedding = embedding_ref[...]
    inverse = lax.rsqrt(jnp.sum(embedding * embedding, axis=1, keepdims=True) + EPS)
    unit = embedding * inverse
    grad_sum = jnp.exp(jnp.full((1, LANES), scale_ref[0], jnp.float32))[:, :1] * total_ref[:, :width]
    along = jnp.sum(unit * grad_sum, axis=1, keepdims=True)
    grads[0] = inverse * (grad_sum - unit * along)
    grads_copy = pltpu.make_async_copy(grads, grads_hbm, sems.at[1])
    grads_copy.start()
    losses_copy.wait()
    grads_copy.wait()


def shards(tower_inputs, image_proj, text_proj, text_lengths, partner, log_scale, bias):
    slices = tower_inputs[0, :, 0, :]
    row_count = slices.shape[0]
    tower = lax.axis_index("tower")
    core = lax.axis_index("mp")
    n_mp = lax.axis_size("mp")
    n_y = lax.axis_size("y")
    n_x = lax.axis_size("x")
    n_z = lax.axis_size("z")
    share = row_count // n_mp
    width = image_proj.shape[1]

    def pair_at(z_at, x_at, y_at):
        return ((z_at * n_x + x_at) * n_y + y_at) * row_count

    core_index = core.astype(jnp.int32).reshape(1)
    kept, sent = lax.cond(
        tower == 0,
        lambda: pooled_partial(image_kernel, core_index, slices, image_proj),
        lambda: pooled_partial(text_kernel, core_index, slices, text_proj, text_lengths),
    )
    embedding = kept + lax.ppermute(sent, "mp", [(0, 1), (1, 0)])
    inverse = lax.rsqrt(jnp.sum(embedding * embedding, axis=1, keepdims=True) + EPS)
    unit = embedding * inverse
    unit_low = unit.astype(jnp.bfloat16)

    first = pair_at(lax.axis_index("z"), lax.axis_index("x"), lax.axis_index("y")) + core * share
    partners = lax.dynamic_slice_in_dim(partner, core * share, share, 0)
    key = jnp.where(tower == 0, partners, first + lax.iota(jnp.int32, share))[:, None]
    column = lax.broadcasted_iota(jnp.int32, (share, LANES), 1)
    coded = (column == key // LOW) | (column == HIGH + key % LOW)
    key_block = coded.astype(jnp.bfloat16)
    own = jnp.concatenate([unit_low, key_block], axis=1)

    near = lax.ppermute(own, "tower", [(0, 1), (1, 0)])
    across = lax.ppermute(own, ("tower", "x"), [(0, 3), (3, 0), (1, 2), (2, 1)])
    other = jnp.concatenate([near, across], axis=0)
    copies = jnp.broadcast_to(other[None], (n_y,) + other.shape)
    held = swap_gather(own, "z")
    other_mine = staggered(copies, "y", (0, n_y // 2))
    other_mine = other_mine.reshape(n_y * n_x * share, width + LANES)
    other_theirs = lax.ppermute(other_mine, "mp", [(0, 1), (1, 0)])
    own_all = in_order(held, "z", share, FIRST_Z, other_mine)

    temper = jnp.exp(log_scale[0])
    own_low = own_all[:, :width]

    def products(rows, columns):
        return lax.dot_general(
            rows, columns, (((1,), (1,)), ((), ())), preferred_element_type=jnp.float32
        )

    def score(others):
        other_low = others[:, :width]
        logits = temper * products(own_low, other_low) + bias[0]
        paired = products(own_all[:, width:], others[:, width:]) > 1.5
        losses = jax.nn.softplus(jnp.where(paired, -logits, logits))
        weights = (jax.nn.sigmoid(logits) - paired.astype(jnp.float32)).astype(jnp.bfloat16)
        grad = jnp.dot(weights, other_low, preferred_element_type=jnp.float32)
        return grad, jnp.sum(losses, axis=1, keepdims=True)

    grad_mine, loss_mine = score(other_mine)
    grad_theirs, loss_theirs = score(other_theirs)
    grad_part = grad_mine + grad_theirs
    loss_part = loss_mine + loss_theirs

    loss_high = lax.reduce_precision(loss_part, 5, 10)
    loss_rest = loss_part - loss_high
    lane = lax.broadcasted_iota(jnp.int32, (n_z * share, LANES), 1)
    loss_block = jnp.where(lane == 0, loss_high, loss_rest).astype(jnp.float16)
    sums = jnp.concatenate([grad_part.astype(jnp.float16), loss_block], axis=1)
    sums = staggered(sums.reshape(n_z, share, width + LANES), "z", FIRST_Z)
    total = jnp.sum(sums.astype(jnp.float32), axis=0)
    vmem = pl.BlockSpec(memory_space=pltpu.VMEM)
    any_space = pl.BlockSpec(memory_space=pl.ANY)
    return pl.pallas_call(
        final_kernel,
        out_shape=(
            jax.ShapeDtypeStruct((1, share, width), jnp.float32),
            jax.ShapeDtypeStruct((1, share), jnp.float32),
        ),
        in_specs=[pl.BlockSpec(memory_space=pltpu.SMEM), vmem, vmem],
        out_specs=(any_space, any_space),
        scratch_shapes=[
            pltpu.VMEM((1, share, width), jnp.float32),
            pltpu.VMEM((1, share), jnp.float32),
            pltpu.SemaphoreType.DMA((2,)),
        ],
        compiler_params=pltpu.CompilerParams(vmem_limit_bytes=8 * 2**20),
    )(log_scale, total, embedding)


def solution(mesh):
    n_tower, n_blk, n_mp = (mesh.shape[name] for name in ("tower", "blk", "mp"))
    n_z, n_x = 8, 2
    grid = Mesh(
        mesh.devices.reshape(n_tower, n_z, n_x, n_blk // (n_z * n_x), n_mp),
        ("tower", "z", "x", "y", "mp"),
    )
    blk = ("z", "x", "y")
    placed = (
        P("tower", blk, "mp", None),
        P("mp", None),
        P("mp", None),
        P(blk),
        P(blk),
        P(),
        P(),
    )
    return jax.shard_map(
        shards,
        mesh=grid,
        in_specs=placed,
        out_specs=(P("tower", blk + ("mp",), None), P("tower", blk + ("mp",))),
        check_vma=False,
    )
```

```python
import jax
import jax.numpy as jnp
from jax import lax
from jax.experimental import pallas as pl
from jax.experimental.pallas import tpu as pltpu
from jax.sharding import Mesh
from jax.sharding import PartitionSpec as P

EPS = 1e-06
PIECE = 256
LANES = 128
HIGH, LOW = 64, 32
SUMS = 3
FIRST_Y = (7, 4)
FIRST_Z = (4, 6)


def project(pooled, weights, copies, core_ref, keep_ref, send_ref):
    total = None
    for copy, first, last in copies:
        copy.wait()
        piece = jnp.dot(
            pooled[:, first:last], weights[first:last, :], preferred_element_type=jnp.float32
        )
        total = piece if total is None else total + piece
    share = keep_ref.shape[0]
    upper, lower = total[:share], total[share:]
    first_core = core_ref[0] == 0
    keep_ref[...] = jnp.where(first_core, upper, lower)
    send_ref[...] = jnp.where(first_core, lower, upper)


def fetch(slices_hbm, weights_hbm, slices, weights, sems):
    depth = weights_hbm.shape[0]
    first_copy = pltpu.make_async_copy(slices_hbm, slices, sems.at[0])
    first_copy.start()
    copies = []
    for place, first in enumerate(range(0, depth, PIECE)):
        last = min(first + PIECE, depth)
        copy = pltpu.make_async_copy(
            weights_hbm.at[first:last], weights.at[first:last], sems.at[1 + place]
        )
        copy.start()
        copies.append((copy, first, min(first + PIECE, weights.shape[0])))
    return first_copy, copies


def image_kernel(core_ref, slices_hbm, weights_hbm, keep_ref, send_ref, slices, weights, sems):
    first_copy, copies = fetch(slices_hbm, weights_hbm, slices, weights, sems)
    width = weights_hbm.shape[0]
    patch_count = slices.shape[1] // width
    first_copy.wait()
    summed = slices[:, :width].astype(jnp.float32)
    for patch in range(1, patch_count):
        summed += slices[:, patch * width : (patch + 1) * width].astype(jnp.float32)
    pooled = (summed / patch_count).astype(jnp.bfloat16)
    project(pooled, weights, copies, core_ref, keep_ref, send_ref)


def text_kernel(
    core_ref, lengths_hbm, slices_hbm, weights_hbm, keep_ref, send_ref, slices, weights, sems, lengths_ref
):
    lengths_copy = pltpu.make_async_copy(lengths_hbm, lengths_ref, sems.at[sems.shape[0] - 1])
    lengths_copy.start()
    first_copy, copies = fetch(slices_hbm, weights_hbm, slices, weights, sems)
    width = weights_hbm.shape[0]
    row_count = slices.shape[0]
    slot_count = slices.shape[1] // width
    padded = weights.shape[0]
    if padded > width:
        weights[width:, :] = jnp.zeros((padded - width, weights.shape[1]), jnp.bfloat16)
    shape = (row_count, 2 * width)
    row = lax.broadcasted_iota(jnp.int32, shape, 0)
    lengths = jnp.zeros(shape, jnp.int32)
    lengths_copy.wait()
    for index in range(row_count):
        lengths = jnp.where(row == index, lengths_ref[index], lengths)
    second = (lax.broadcasted_iota(jnp.int32, shape, 1) >= width).astype(jnp.int32)
    left = lengths - second
    first_copy.wait()
    summed = jnp.zeros(shape, jnp.float32)
    for slot in range(0, slot_count, 2):
        piece = slices[:, slot * width : (slot + 2) * width].astype(jnp.float32)
        summed += jnp.where(slot < left, piece, 0.0)
    summed = summed + pltpu.roll(summed, width, 1)
    pooled = (summed / lengths.astype(jnp.float32)).astype(jnp.bfloat16)
    project(pooled, weights, copies, core_ref, keep_ref, send_ref)


def pooled_partial(kernel, core_index, slices, weights, lengths=None):
    row_count = slices.shape[0]
    depth, width = weights.shape
    padded = -(-depth // LANES) * LANES
    pieces = -(-depth // PIECE)
    any_space = pl.BlockSpec(memory_space=pl.ANY)
    half = jax.ShapeDtypeStruct((row_count // 2, width), jnp.float32)
    given = (slices, weights) if lengths is None else (lengths, slices, weights)
    scratch = [
        pltpu.VMEM(slices.shape, jnp.bfloat16),
        pltpu.VMEM((padded, width), jnp.bfloat16),
        pltpu.SemaphoreType.DMA((2 + pieces,)),
    ]
    if lengths is not None:
        scratch.append(pltpu.SMEM(lengths.shape, jnp.int32))
    return pl.pallas_call(
        kernel,
        out_shape=(half, half),
        in_specs=[pl.BlockSpec(memory_space=pltpu.SMEM)] + [any_space] * len(given),
        out_specs=(pl.BlockSpec(memory_space=pltpu.VMEM),) * 2,
        scratch_shapes=scratch,
        compiler_params=pltpu.CompilerParams(vmem_limit_bytes=32 * 2**20),
    )(core_index, *given)


def staggered(blocks, axis, firsts):
    members = lax.axis_size(axis)
    cores = lax.axis_size("mp")
    groups = [
        [(at + firsts[core]) % members * cores + core for at in range(members)]
        for core in range(cores)
    ]
    return lax.all_to_all(blocks, (axis, "mp"), 0, 0, axis_index_groups=groups, tiled=True)


def swap_gather(block, axis):
    members = lax.axis_size(axis)
    half = members // 2

    def brought(value, across):
        return lax.ppermute(value, axis, [(index, index ^ across) for index in range(members)])

    pair = jnp.concatenate([block, brought(block, half)], axis=0)
    wide = pair.astype(jnp.float32)
    passed = jnp.sum(wide, axis=0, keepdims=True)
    for _ in range(SUMS - 1):
        passed = jnp.sum(wide * passed, axis=0, keepdims=True)
    pair = pair + (passed * 0).astype(pair.dtype)
    return jnp.concatenate([pair] + [brought(pair, across) for across in range(1, half)], axis=0)


def in_order(held, axis, size, firsts, last):
    members = lax.axis_size(axis)
    place = lax.broadcasted_iota(jnp.int32, (members * size, members * size), 0)
    slot = lax.broadcasted_iota(jnp.int32, (members * size, members * size), 1)
    number = slot // size
    came_from = lax.axis_index(axis) ^ (number // 2 + (number % 2) * (members // 2))
    first = jnp.where(lax.axis_index("mp") == 0, firsts[0], firsts[1])
    member = (place // size + first) % members
    moves = (member == came_from) & (place % size == slot % size)
    moves = moves.astype(held.dtype) + last[: members * size, : members * size] * 0
    ordered = jnp.dot(moves, held, preferred_element_type=jnp.float32)
    return ordered.astype(held.dtype)


def final_kernel(scale_ref, total_ref, embedding_ref, grads_hbm, losses_hbm, grads, losses, sems):
    share, width = embedding_ref.shape
    loss = total_ref[:, width : width + 1] + total_ref[:, width + 1 : width + 2]
    row = lax.broadcasted_iota(jnp.int32, (share, LANES), 0)
    column = lax.broadcasted_iota(jnp.int32, (share, LANES), 1)
    diagonal = jnp.where(row == column, jnp.broadcast_to(loss, (share, LANES)), 0.0)
    losses[...] = jnp.sum(diagonal, axis=0, keepdims=True)[:, :share]
    losses_copy = pltpu.make_async_copy(losses, losses_hbm, sems.at[0])
    losses_copy.start()
    embedding = embedding_ref[...]
    inverse = lax.rsqrt(jnp.sum(embedding * embedding, axis=1, keepdims=True) + EPS)
    unit = embedding * inverse
    grad_sum = jnp.exp(jnp.full((1, LANES), scale_ref[0], jnp.float32))[:, :1] * total_ref[:, :width]
    along = jnp.sum(unit * grad_sum, axis=1, keepdims=True)
    grads[0] = inverse * (grad_sum - unit * along)
    grads_copy = pltpu.make_async_copy(grads, grads_hbm, sems.at[1])
    grads_copy.start()
    losses_copy.wait()
    grads_copy.wait()


def shards(tower_inputs, image_proj, text_proj, text_lengths, partner, log_scale, bias):
    slices = tower_inputs[0, :, 0, :]
    row_count = slices.shape[0]
    tower = lax.axis_index("tower")
    core = lax.axis_index("mp")
    n_mp = lax.axis_size("mp")
    n_y = lax.axis_size("y")
    n_x = lax.axis_size("x")
    n_z = lax.axis_size("z")
    share = row_count // n_mp
    width = image_proj.shape[1]

    def pair_at(z_at, x_at, y_at):
        return ((z_at * n_x + x_at) * n_y + y_at) * row_count

    core_index = core.astype(jnp.int32).reshape(1)
    kept, sent = lax.cond(
        tower == 0,
        lambda: pooled_partial(image_kernel, core_index, slices, image_proj),
        lambda: pooled_partial(text_kernel, core_index, slices, text_proj, text_lengths),
    )
    embedding = kept + lax.ppermute(sent, "mp", [(0, 1), (1, 0)])
    inverse = lax.rsqrt(jnp.sum(embedding * embedding, axis=1, keepdims=True) + EPS)
    unit = embedding * inverse
    unit_low = unit.astype(jnp.bfloat16)

    first = pair_at(lax.axis_index("z"), lax.axis_index("x"), lax.axis_index("y")) + core * share
    partners = lax.dynamic_slice_in_dim(partner, core * share, share, 0)
    key = jnp.where(tower == 0, partners, first + lax.iota(jnp.int32, share))[:, None]
    column = lax.broadcasted_iota(jnp.int32, (share, LANES), 1)
    coded = (column == key // LOW) | (column == HIGH + key % LOW)
    key_block = coded.astype(jnp.bfloat16)
    own = jnp.concatenate([unit_low, key_block], axis=1)

    near = lax.ppermute(own, "tower", [(0, 1), (1, 0)])
    across = lax.ppermute(own, ("tower", "x"), [(0, 3), (3, 0), (1, 2), (2, 1)])
    temper = jnp.exp(log_scale[0])
    other = jnp.concatenate([near, across], axis=0) + (temper * 0).astype(near.dtype)
    copies = jnp.broadcast_to(other[None], (n_y,) + other.shape)
    held = swap_gather(own, "z")
    other_mine = staggered(copies, "y", FIRST_Y)
    other_mine = other_mine.reshape(n_y * n_x * share, width + LANES)
    other_theirs = lax.ppermute(other_mine, "mp", [(0, 1), (1, 0)])
    own_all = in_order(held, "z", share, FIRST_Z, other_mine)

    own_low = own_all[:, :width]

    def products(rows, columns):
        return lax.dot_general(
            rows, columns, (((1,), (1,)), ((), ())), preferred_element_type=jnp.float32
        )

    def score(others):
        other_low = others[:, :width]
        logits = temper * products(own_low, other_low) + bias[0]
        paired = products(own_all[:, width:], others[:, width:]) > 1.5
        losses = jax.nn.softplus(jnp.where(paired, -logits, logits))
        weights = (jax.nn.sigmoid(logits) - paired.astype(jnp.float32)).astype(jnp.bfloat16)
        grad = jnp.dot(weights, other_low, preferred_element_type=jnp.float32)
        return grad, jnp.sum(losses, axis=1, keepdims=True)

    grad_mine, loss_mine = score(other_mine)
    grad_theirs, loss_theirs = score(other_theirs)
    grad_part = grad_mine + grad_theirs
    loss_part = loss_mine + loss_theirs

    loss_high = lax.reduce_precision(loss_part, 5, 10)
    loss_rest = loss_part - loss_high
    lane = lax.broadcasted_iota(jnp.int32, (n_z * share, LANES), 1)
    loss_block = jnp.where(lane == 0, loss_high, loss_rest).astype(jnp.float16)
    sums = jnp.concatenate([grad_part.astype(jnp.float16), loss_block], axis=1)
    sums = staggered(sums.reshape(n_z, share, width + LANES), "z", FIRST_Z)
    total = jnp.sum(sums.astype(jnp.float32), axis=0)
    vmem = pl.BlockSpec(memory_space=pltpu.VMEM)
    any_space = pl.BlockSpec(memory_space=pl.ANY)
    return pl.pallas_call(
        final_kernel,
        out_shape=(
            jax.ShapeDtypeStruct((1, share, width), jnp.float32),
            jax.ShapeDtypeStruct((1, share), jnp.float32),
        ),
        in_specs=[pl.BlockSpec(memory_space=pltpu.SMEM), vmem, vmem],
        out_specs=(any_space, any_space),
        scratch_shapes=[
            pltpu.VMEM((1, share, width), jnp.float32),
            pltpu.VMEM((1, share), jnp.float32),
            pltpu.SemaphoreType.DMA((2,)),
        ],
        compiler_params=pltpu.CompilerParams(vmem_limit_bytes=8 * 2**20),
    )(log_scale, total, embedding)


def solution(mesh):
    n_tower, n_blk, n_mp = (mesh.shape[name] for name in ("tower", "blk", "mp"))
    n_z, n_x = 8, 2
    grid = Mesh(
        mesh.devices.reshape(n_tower, n_z, n_x, n_blk // (n_z * n_x), n_mp),
        ("tower", "z", "x", "y", "mp"),
    )
    blk = ("z", "x", "y")
    placed = (
        P("tower", blk, "mp", None),
        P("mp", None),
        P("mp", None),
        P(blk),
        P(blk),
        P(),
        P(),
    )
    return jax.shard_map(
        shards,
        mesh=grid,
        in_specs=placed,
        out_specs=(P("tower", blk + ("mp",), None), P("tower", blk + ("mp",))),
        check_vma=False,
    )
```

```python
import jax
import jax.numpy as jnp
from jax import lax
from jax.experimental import pallas as pl
from jax.experimental.pallas import tpu as pltpu
from jax.sharding import Mesh
from jax.sharding import PartitionSpec as P

EPS = 1e-06
PIECE = 256
LANES = 128
HIGH, LOW = 64, 32
SUMS = 3
FIRST_Y = (7, 4)
FIRST_Z = (4, 6)


def project(pooled, weights, copies, core_ref, keep_ref, send_ref):
    total = None
    for copy, first, last in copies:
        copy.wait()
        piece = jnp.dot(
            pooled[:, first:last], weights[first:last, :], preferred_element_type=jnp.float32
        )
        total = piece if total is None else total + piece
    share = keep_ref.shape[0]
    upper, lower = total[:share], total[share:]
    first_core = core_ref[0] == 0
    keep_ref[...] = jnp.where(first_core, upper, lower)
    send_ref[...] = jnp.where(first_core, lower, upper)


def fetch(slices_hbm, weights_hbm, slices, weights, sems):
    depth = weights_hbm.shape[0]
    first_copy = pltpu.make_async_copy(slices_hbm, slices, sems.at[0])
    first_copy.start()
    copies = []
    for place, first in enumerate(range(0, depth, PIECE)):
        last = min(first + PIECE, depth)
        copy = pltpu.make_async_copy(
            weights_hbm.at[first:last], weights.at[first:last], sems.at[1 + place]
        )
        copy.start()
        copies.append((copy, first, min(first + PIECE, weights.shape[0])))
    return first_copy, copies


def image_kernel(core_ref, slices_hbm, weights_hbm, keep_ref, send_ref, slices, weights, sems):
    first_copy, copies = fetch(slices_hbm, weights_hbm, slices, weights, sems)
    width = weights_hbm.shape[0]
    patch_count = slices.shape[1] // width
    first_copy.wait()
    summed = slices[:, :width].astype(jnp.float32)
    for patch in range(1, patch_count):
        summed += slices[:, patch * width : (patch + 1) * width].astype(jnp.float32)
    pooled = (summed / patch_count).astype(jnp.bfloat16)
    project(pooled, weights, copies, core_ref, keep_ref, send_ref)


def text_kernel(
    core_ref, lengths_hbm, slices_hbm, weights_hbm, keep_ref, send_ref, slices, weights, sems, lengths_ref
):
    lengths_copy = pltpu.make_async_copy(lengths_hbm, lengths_ref, sems.at[sems.shape[0] - 1])
    lengths_copy.start()
    first_copy, copies = fetch(slices_hbm, weights_hbm, slices, weights, sems)
    width = weights_hbm.shape[0]
    row_count = slices.shape[0]
    slot_count = slices.shape[1] // width
    padded = weights.shape[0]
    if padded > width:
        weights[width:, :] = jnp.zeros((padded - width, weights.shape[1]), jnp.bfloat16)
    shape = (row_count, 2 * width)
    row = lax.broadcasted_iota(jnp.int32, shape, 0)
    lengths = jnp.zeros(shape, jnp.int32)
    lengths_copy.wait()
    for index in range(row_count):
        lengths = jnp.where(row == index, lengths_ref[index], lengths)
    second = (lax.broadcasted_iota(jnp.int32, shape, 1) >= width).astype(jnp.int32)
    left = lengths - second
    first_copy.wait()
    summed = jnp.zeros(shape, jnp.float32)
    for slot in range(0, slot_count, 2):
        piece = slices[:, slot * width : (slot + 2) * width].astype(jnp.float32)
        summed += jnp.where(slot < left, piece, 0.0)
    summed = summed + pltpu.roll(summed, width, 1)
    pooled = (summed / lengths.astype(jnp.float32)).astype(jnp.bfloat16)
    project(pooled, weights, copies, core_ref, keep_ref, send_ref)


def pooled_partial(kernel, core_index, slices, weights, lengths=None):
    row_count = slices.shape[0]
    depth, width = weights.shape
    padded = -(-depth // LANES) * LANES
    pieces = -(-depth // PIECE)
    any_space = pl.BlockSpec(memory_space=pl.ANY)
    half = jax.ShapeDtypeStruct((row_count // 2, width), jnp.float32)
    given = (slices, weights) if lengths is None else (lengths, slices, weights)
    scratch = [
        pltpu.VMEM(slices.shape, jnp.bfloat16),
        pltpu.VMEM((padded, width), jnp.bfloat16),
        pltpu.SemaphoreType.DMA((2 + pieces,)),
    ]
    if lengths is not None:
        scratch.append(pltpu.SMEM(lengths.shape, jnp.int32))
    return pl.pallas_call(
        kernel,
        out_shape=(half, half),
        in_specs=[pl.BlockSpec(memory_space=pltpu.SMEM)] + [any_space] * len(given),
        out_specs=(pl.BlockSpec(memory_space=pltpu.VMEM),) * 2,
        scratch_shapes=scratch,
        compiler_params=pltpu.CompilerParams(vmem_limit_bytes=32 * 2**20),
    )(core_index, *given)


def staggered(blocks, axis, firsts):
    members = lax.axis_size(axis)
    cores = lax.axis_size("mp")
    groups = [
        [(at + firsts[core]) % members * cores + core for at in range(members)]
        for core in range(cores)
    ]
    return lax.all_to_all(blocks, (axis, "mp"), 0, 0, axis_index_groups=groups, tiled=True)


def ring_partners(index, members):
    return (index ^ 1, ((index + 1) ^ 1) + members - 1 & members - 1, index ^ 2)


def swap_gather(block, axis):
    members = lax.axis_size(axis)
    half = members // 2

    def brought(value, partners):
        return lax.ppermute(value, axis, list(enumerate(partners)))

    pair = jnp.concatenate([block, brought(block, [at ^ half for at in range(members)])], axis=0)
    wide = pair.astype(jnp.float32)
    passed = jnp.sum(wide, axis=0, keepdims=True)
    for _ in range(SUMS - 1):
        passed = jnp.sum(wide * passed, axis=0, keepdims=True)
    pair = pair + (passed * 0).astype(pair.dtype)
    table = [ring_partners(at, members) for at in range(members)]
    near = [brought(pair, [row[step] for row in table]) for step in range(half - 1)]
    return jnp.concatenate([pair] + near, axis=0)


def in_order(held, axis, size, firsts, last):
    members = lax.axis_size(axis)
    place = lax.broadcasted_iota(jnp.int32, (members * size, members * size), 0)
    slot = lax.broadcasted_iota(jnp.int32, (members * size, members * size), 1)
    number = slot // size
    me = lax.axis_index(axis)
    came_from = me
    for step, partner in enumerate(ring_partners(me, members)):
        came_from = jnp.where(number // 2 == step + 1, partner, came_from)
    came_from = came_from ^ ((number % 2) * (members // 2))
    first = jnp.where(lax.axis_index("mp") == 0, firsts[0], firsts[1])
    member = (place // size + first) % members
    moves = (member == came_from) & (place % size == slot % size)
    moves = moves.astype(held.dtype) + last[: members * size, : members * size] * 0
    ordered = jnp.dot(moves, held, preferred_element_type=jnp.float32)
    return ordered.astype(held.dtype)


def final_kernel(scale_ref, total_ref, embedding_ref, grads_hbm, losses_hbm, grads, losses, sems):
    share, width = embedding_ref.shape
    loss = total_ref[:, width : width + 1] + total_ref[:, width + 1 : width + 2]
    row = lax.broadcasted_iota(jnp.int32, (share, LANES), 0)
    column = lax.broadcasted_iota(jnp.int32, (share, LANES), 1)
    diagonal = jnp.where(row == column, jnp.broadcast_to(loss, (share, LANES)), 0.0)
    losses[...] = jnp.sum(diagonal, axis=0, keepdims=True)[:, :share]
    losses_copy = pltpu.make_async_copy(losses, losses_hbm, sems.at[0])
    losses_copy.start()
    embedding = embedding_ref[...]
    inverse = lax.rsqrt(jnp.sum(embedding * embedding, axis=1, keepdims=True) + EPS)
    unit = embedding * inverse
    grad_sum = jnp.exp(jnp.full((1, LANES), scale_ref[0], jnp.float32))[:, :1] * total_ref[:, :width]
    along = jnp.sum(unit * grad_sum, axis=1, keepdims=True)
    grads[0] = inverse * (grad_sum - unit * along)
    grads_copy = pltpu.make_async_copy(grads, grads_hbm, sems.at[1])
    grads_copy.start()
    losses_copy.wait()
    grads_copy.wait()


def shards(tower_inputs, image_proj, text_proj, text_lengths, partner, log_scale, bias):
    slices = tower_inputs[0, :, 0, :]
    row_count = slices.shape[0]
    tower = lax.axis_index("tower")
    core = lax.axis_index("mp")
    n_mp = lax.axis_size("mp")
    n_y = lax.axis_size("y")
    n_x = lax.axis_size("x")
    n_z = lax.axis_size("z")
    share = row_count // n_mp
    width = image_proj.shape[1]

    def pair_at(z_at, x_at, y_at):
        return ((z_at * n_x + x_at) * n_y + y_at) * row_count

    core_index = core.astype(jnp.int32).reshape(1)
    kept, sent = lax.cond(
        tower == 0,
        lambda: pooled_partial(image_kernel, core_index, slices, image_proj),
        lambda: pooled_partial(text_kernel, core_index, slices, text_proj, text_lengths),
    )
    embedding = kept + lax.ppermute(sent, "mp", [(0, 1), (1, 0)])
    inverse = lax.rsqrt(jnp.sum(embedding * embedding, axis=1, keepdims=True) + EPS)
    unit = embedding * inverse
    unit_low = unit.astype(jnp.bfloat16)

    first = pair_at(lax.axis_index("z"), lax.axis_index("x"), lax.axis_index("y")) + core * share
    partners = lax.dynamic_slice_in_dim(partner, core * share, share, 0)
    key = jnp.where(tower == 0, partners, first + lax.iota(jnp.int32, share))[:, None]
    column = lax.broadcasted_iota(jnp.int32, (share, LANES), 1)
    coded = (column == key // LOW) | (column == HIGH + key % LOW)
    key_block = coded.astype(jnp.bfloat16)
    own = jnp.concatenate([unit_low, key_block], axis=1)

    near = lax.ppermute(own, "tower", [(0, 1), (1, 0)])
    across = lax.ppermute(own, ("tower", "x"), [(0, 3), (3, 0), (1, 2), (2, 1)])
    temper = jnp.exp(log_scale[0])
    other = jnp.concatenate([near, across], axis=0) + (temper * 0).astype(near.dtype)
    copies = jnp.broadcast_to(other[None], (n_y,) + other.shape)
    held = swap_gather(own, "z")
    other_mine = staggered(copies, "y", FIRST_Y)
    other_mine = other_mine.reshape(n_y * n_x * share, width + LANES)
    other_theirs = lax.ppermute(other_mine, "mp", [(0, 1), (1, 0)])
    own_all = in_order(held, "z", share, FIRST_Z, other_mine)

    own_low = own_all[:, :width]

    def products(rows, columns):
        return lax.dot_general(
            rows, columns, (((1,), (1,)), ((), ())), preferred_element_type=jnp.float32
        )

    def score(others):
        other_low = others[:, :width]
        logits = temper * products(own_low, other_low) + bias[0]
        paired = products(own_all[:, width:], others[:, width:]) > 1.5
        losses = jax.nn.softplus(jnp.where(paired, -logits, logits))
        weights = (jax.nn.sigmoid(logits) - paired.astype(jnp.float32)).astype(jnp.bfloat16)
        grad = jnp.dot(weights, other_low, preferred_element_type=jnp.float32)
        return grad, jnp.sum(losses, axis=1, keepdims=True)

    grad_mine, loss_mine = score(other_mine)
    grad_theirs, loss_theirs = score(other_theirs)
    grad_part = grad_mine + grad_theirs
    loss_part = loss_mine + loss_theirs

    loss_high = lax.reduce_precision(loss_part, 5, 10)
    loss_rest = loss_part - loss_high
    lane = lax.broadcasted_iota(jnp.int32, (n_z * share, LANES), 1)
    loss_block = jnp.where(lane == 0, loss_high, loss_rest).astype(jnp.float16)
    sums = jnp.concatenate([grad_part.astype(jnp.float16), loss_block], axis=1)
    sums = staggered(sums.reshape(n_z, share, width + LANES), "z", FIRST_Z)
    total = jnp.sum(sums.astype(jnp.float32), axis=0)
    vmem = pl.BlockSpec(memory_space=pltpu.VMEM)
    any_space = pl.BlockSpec(memory_space=pl.ANY)
    return pl.pallas_call(
        final_kernel,
        out_shape=(
            jax.ShapeDtypeStruct((1, share, width), jnp.float32),
            jax.ShapeDtypeStruct((1, share), jnp.float32),
        ),
        in_specs=[pl.BlockSpec(memory_space=pltpu.SMEM), vmem, vmem],
        out_specs=(any_space, any_space),
        scratch_shapes=[
            pltpu.VMEM((1, share, width), jnp.float32),
            pltpu.VMEM((1, share), jnp.float32),
            pltpu.SemaphoreType.DMA((2,)),
        ],
        compiler_params=pltpu.CompilerParams(vmem_limit_bytes=8 * 2**20),
    )(log_scale, total, embedding)


def solution(mesh):
    n_tower, n_blk, n_mp = (mesh.shape[name] for name in ("tower", "blk", "mp"))
    n_z, n_x = 8, 2
    grid = Mesh(
        mesh.devices.reshape(n_tower, n_z, n_x, n_blk // (n_z * n_x), n_mp),
        ("tower", "z", "x", "y", "mp"),
    )
    blk = ("z", "x", "y")
    placed = (
        P("tower", blk, "mp", None),
        P("mp", None),
        P("mp", None),
        P(blk),
        P(blk),
        P(),
        P(),
    )
    return jax.shard_map(
        shards,
        mesh=grid,
        in_specs=placed,
        out_specs=(P("tower", blk + ("mp",), None), P("tower", blk + ("mp",))),
        check_vma=False,
    )
```

```python
import jax
import jax.numpy as jnp
from jax import lax
from jax.experimental import pallas as pl
from jax.experimental.pallas import tpu as pltpu
from jax.sharding import Mesh
from jax.sharding import PartitionSpec as P

EPS = 1e-06
PIECE = 256
LANES = 128
HIGH, LOW = 64, 32
SUMS = 3
FIRST_Y = (7, 4)
FIRST_Z = (4, 6)


def project(pooled, weights, copies, core_ref, keep_ref, send_ref):
    total = None
    for copy, first, last in copies:
        copy.wait()
        piece = jnp.dot(
            pooled[:, first:last], weights[first:last, :], preferred_element_type=jnp.float32
        )
        total = piece if total is None else total + piece
    share = keep_ref.shape[0]
    upper, lower = total[:share], total[share:]
    first_core = core_ref[0] == 0
    keep_ref[...] = jnp.where(first_core, upper, lower)
    send_ref[...] = jnp.where(first_core, lower, upper)


def fetch(slices_hbm, weights_hbm, slices, weights, sems):
    depth = weights_hbm.shape[0]
    first_copy = pltpu.make_async_copy(slices_hbm, slices, sems.at[0])
    first_copy.start()
    copies = []
    for place, first in enumerate(range(0, depth, PIECE)):
        last = min(first + PIECE, depth)
        copy = pltpu.make_async_copy(
            weights_hbm.at[first:last], weights.at[first:last], sems.at[1 + place]
        )
        copy.start()
        copies.append((copy, first, min(first + PIECE, weights.shape[0])))
    return first_copy, copies


def image_kernel(core_ref, slices_hbm, weights_hbm, keep_ref, send_ref, slices, weights, sems):
    first_copy, copies = fetch(slices_hbm, weights_hbm, slices, weights, sems)
    width = weights_hbm.shape[0]
    patch_count = slices.shape[1] // width
    first_copy.wait()
    summed = slices[:, :width].astype(jnp.float32)
    for patch in range(1, patch_count):
        summed += slices[:, patch * width : (patch + 1) * width].astype(jnp.float32)
    pooled = (summed / patch_count).astype(jnp.bfloat16)
    project(pooled, weights, copies, core_ref, keep_ref, send_ref)


def text_kernel(
    core_ref, lengths_hbm, slices_hbm, weights_hbm, keep_ref, send_ref, slices, weights, sems, lengths_ref
):
    lengths_copy = pltpu.make_async_copy(lengths_hbm, lengths_ref, sems.at[sems.shape[0] - 1])
    lengths_copy.start()
    first_copy, copies = fetch(slices_hbm, weights_hbm, slices, weights, sems)
    width = weights_hbm.shape[0]
    row_count = slices.shape[0]
    slot_count = slices.shape[1] // width
    padded = weights.shape[0]
    if padded > width:
        weights[width:, :] = jnp.zeros((padded - width, weights.shape[1]), jnp.bfloat16)
    shape = (row_count, 2 * width)
    row = lax.broadcasted_iota(jnp.int32, shape, 0)
    lengths = jnp.zeros(shape, jnp.int32)
    lengths_copy.wait()
    for index in range(row_count):
        lengths = jnp.where(row == index, lengths_ref[index], lengths)
    second = (lax.broadcasted_iota(jnp.int32, shape, 1) >= width).astype(jnp.int32)
    left = lengths - second
    first_copy.wait()
    summed = jnp.zeros(shape, jnp.float32)
    for slot in range(0, slot_count, 2):
        piece = slices[:, slot * width : (slot + 2) * width].astype(jnp.float32)
        summed += jnp.where(slot < left, piece, 0.0)
    summed = summed + pltpu.roll(summed, width, 1)
    pooled = (summed / lengths.astype(jnp.float32)).astype(jnp.bfloat16)
    project(pooled, weights, copies, core_ref, keep_ref, send_ref)


def pooled_partial(kernel, core_index, slices, weights, lengths=None):
    row_count = slices.shape[0]
    depth, width = weights.shape
    padded = -(-depth // LANES) * LANES
    pieces = -(-depth // PIECE)
    any_space = pl.BlockSpec(memory_space=pl.ANY)
    half = jax.ShapeDtypeStruct((row_count // 2, width), jnp.float32)
    given = (slices, weights) if lengths is None else (lengths, slices, weights)
    scratch = [
        pltpu.VMEM(slices.shape, jnp.bfloat16),
        pltpu.VMEM((padded, width), jnp.bfloat16),
        pltpu.SemaphoreType.DMA((2 + pieces,)),
    ]
    if lengths is not None:
        scratch.append(pltpu.SMEM(lengths.shape, jnp.int32))
    return pl.pallas_call(
        kernel,
        out_shape=(half, half),
        in_specs=[pl.BlockSpec(memory_space=pltpu.SMEM)] + [any_space] * len(given),
        out_specs=(pl.BlockSpec(memory_space=pltpu.VMEM),) * 2,
        scratch_shapes=scratch,
        compiler_params=pltpu.CompilerParams(vmem_limit_bytes=32 * 2**20),
    )(core_index, *given)


def staggered(blocks, axis, firsts):
    members = lax.axis_size(axis)
    cores = lax.axis_size("mp")
    groups = [
        [(at + firsts[core]) % members * cores + core for at in range(members)]
        for core in range(cores)
    ]
    return lax.all_to_all(blocks, (axis, "mp"), 0, 0, axis_index_groups=groups, tiled=True)


def swap_gather(block, axis):
    members = lax.axis_size(axis)
    half = members // 2

    def brought(value, across):
        return lax.ppermute(value, axis, [(index, index ^ across) for index in range(members)])

    pair = jnp.concatenate([block, brought(block, half)], axis=0)
    wide = pair.astype(jnp.float32)
    passed = jnp.sum(wide, axis=0, keepdims=True)
    for _ in range(SUMS - 1):
        passed = jnp.sum(wide * passed, axis=0, keepdims=True)
    pair = pair + (passed * 0).astype(pair.dtype)
    return jnp.concatenate([pair] + [brought(pair, across) for across in range(1, half)], axis=0)


def in_order(held, axis, size, firsts, last):
    members = lax.axis_size(axis)
    place = lax.broadcasted_iota(jnp.int32, (members * size, members * size), 0)
    slot = lax.broadcasted_iota(jnp.int32, (members * size, members * size), 1)
    number = slot // size
    came_from = lax.axis_index(axis) ^ (number // 2 + (number % 2) * (members // 2))
    first = jnp.where(lax.axis_index("mp") == 0, firsts[0], firsts[1])
    member = (place // size + first) % members
    moves = (member == came_from) & (place % size == slot % size)
    moves = moves.astype(held.dtype) + last[: members * size, : members * size] * 0
    ordered = jnp.dot(moves, held, preferred_element_type=jnp.float32)
    return ordered.astype(held.dtype)


def final_kernel(scale_ref, total_ref, embedding_ref, grads_hbm, losses_hbm, grads, losses, sems):
    share, width = embedding_ref.shape
    loss = total_ref[:, width : width + 1] + total_ref[:, width + 1 : width + 2]
    row = lax.broadcasted_iota(jnp.int32, (share, LANES), 0)
    column = lax.broadcasted_iota(jnp.int32, (share, LANES), 1)
    diagonal = jnp.where(row == column, jnp.broadcast_to(loss, (share, LANES)), 0.0)
    losses[...] = jnp.sum(diagonal, axis=0, keepdims=True)[:, :share]
    losses_copy = pltpu.make_async_copy(losses, losses_hbm, sems.at[0])
    losses_copy.start()
    embedding = embedding_ref[...]
    inverse = lax.rsqrt(jnp.sum(embedding * embedding, axis=1, keepdims=True) + EPS)
    unit = embedding * inverse
    grad_sum = jnp.exp(jnp.full((1, LANES), scale_ref[0], jnp.float32))[:, :1] * total_ref[:, :width]
    along = jnp.sum(unit * grad_sum, axis=1, keepdims=True)
    grads[0] = inverse * (grad_sum - unit * along)
    grads_copy = pltpu.make_async_copy(grads, grads_hbm, sems.at[1])
    grads_copy.start()
    losses_copy.wait()
    grads_copy.wait()


def shards(tower_inputs, image_proj, text_proj, text_lengths, partner, log_scale, bias):
    slices = tower_inputs[0, :, 0, :]
    row_count = slices.shape[0]
    tower = lax.axis_index("tower")
    core = lax.axis_index("mp")
    n_mp = lax.axis_size("mp")
    n_y = lax.axis_size("y")
    n_x = lax.axis_size("x")
    n_z = lax.axis_size("z")
    share = row_count // n_mp
    width = image_proj.shape[1]

    def pair_at(z_at, x_at, y_at):
        return ((z_at * n_x + x_at) * n_y + y_at) * row_count

    core_index = core.astype(jnp.int32).reshape(1)
    kept, sent = lax.cond(
        tower == 0,
        lambda: pooled_partial(image_kernel, core_index, slices, image_proj),
        lambda: pooled_partial(text_kernel, core_index, slices, text_proj, text_lengths),
    )
    embedding = kept + lax.ppermute(sent, "mp", [(0, 1), (1, 0)])
    inverse = lax.rsqrt(jnp.sum(embedding * embedding, axis=1, keepdims=True) + EPS)
    unit = embedding * inverse
    unit_low = unit.astype(jnp.bfloat16)

    first = pair_at(lax.axis_index("z"), lax.axis_index("x"), lax.axis_index("y")) + core * share
    partners = lax.dynamic_slice_in_dim(partner, core * share, share, 0)
    key = jnp.where(tower == 0, partners, first + lax.iota(jnp.int32, share))[:, None]
    column = lax.broadcasted_iota(jnp.int32, (share, LANES), 1)
    coded = (column == key // LOW) | (column == HIGH + key % LOW)
    key_block = coded.astype(jnp.bfloat16)
    own = jnp.concatenate([unit_low, key_block], axis=1)

    near = lax.ppermute(own, "tower", [(0, 1), (1, 0)])
    across = lax.ppermute(own, ("tower", "x"), [(0, 3), (3, 0), (1, 2), (2, 1)])
    temper, offset = jnp.exp(log_scale[0]), bias[0]
    other = jnp.concatenate([near, across], axis=0) + ((temper + offset) * 0).astype(near.dtype)
    copies = jnp.broadcast_to(other[None], (n_y,) + other.shape)
    held = swap_gather(own, "z")
    other_mine = staggered(copies, "y", FIRST_Y)
    other_mine = other_mine.reshape(n_y * n_x * share, width + LANES)
    other_theirs = lax.ppermute(other_mine, "mp", [(0, 1), (1, 0)])
    own_all = in_order(held, "z", share, FIRST_Z, other_mine)

    own_low = own_all[:, :width]

    def products(rows, columns):
        return lax.dot_general(
            rows, columns, (((1,), (1,)), ((), ())), preferred_element_type=jnp.float32
        )

    def score(others):
        other_low = others[:, :width]
        logits = temper * products(own_low, other_low) + offset
        paired = products(own_all[:, width:], others[:, width:]) > 1.5
        losses = jax.nn.softplus(jnp.where(paired, -logits, logits))
        weights = (jax.nn.sigmoid(logits) - paired.astype(jnp.float32)).astype(jnp.bfloat16)
        grad = jnp.dot(weights, other_low, preferred_element_type=jnp.float32)
        return grad, jnp.sum(losses, axis=1, keepdims=True)

    grad_mine, loss_mine = score(other_mine)
    grad_theirs, loss_theirs = score(other_theirs)
    grad_part = grad_mine + grad_theirs
    loss_part = loss_mine + loss_theirs

    loss_high = lax.reduce_precision(loss_part, 5, 10)
    loss_rest = loss_part - loss_high
    lane = lax.broadcasted_iota(jnp.int32, (n_z * share, LANES), 1)
    loss_block = jnp.where(lane == 0, loss_high, loss_rest).astype(jnp.float16)
    sums = jnp.concatenate([grad_part.astype(jnp.float16), loss_block], axis=1)
    sums = staggered(sums.reshape(n_z, share, width + LANES), "z", FIRST_Z)
    total = jnp.sum(sums.astype(jnp.float32), axis=0)
    vmem = pl.BlockSpec(memory_space=pltpu.VMEM)
    any_space = pl.BlockSpec(memory_space=pl.ANY)
    return pl.pallas_call(
        final_kernel,
        out_shape=(
            jax.ShapeDtypeStruct((1, share, width), jnp.float32),
            jax.ShapeDtypeStruct((1, share), jnp.float32),
        ),
        in_specs=[pl.BlockSpec(memory_space=pltpu.SMEM), vmem, vmem],
        out_specs=(any_space, any_space),
        scratch_shapes=[
            pltpu.VMEM((1, share, width), jnp.float32),
            pltpu.VMEM((1, share), jnp.float32),
            pltpu.SemaphoreType.DMA((2,)),
        ],
        compiler_params=pltpu.CompilerParams(vmem_limit_bytes=8 * 2**20),
    )(log_scale, total, embedding)


def solution(mesh):
    n_tower, n_blk, n_mp = (mesh.shape[name] for name in ("tower", "blk", "mp"))
    n_z, n_x = 8, 2
    grid = Mesh(
        mesh.devices.reshape(n_tower, n_z, n_x, n_blk // (n_z * n_x), n_mp),
        ("tower", "z", "x", "y", "mp"),
    )
    blk = ("z", "x", "y")
    placed = (
        P("tower", blk, "mp", None),
        P("mp", None),
        P("mp", None),
        P(blk),
        P(blk),
        P(),
        P(),
    )
    return jax.shard_map(
        shards,
        mesh=grid,
        in_specs=placed,
        out_specs=(P("tower", blk + ("mp",), None), P("tower", blk + ("mp",))),
        check_vma=False,
    )
```

```python
import jax
import jax.numpy as jnp
from jax import lax
from jax.experimental import pallas as pl
from jax.experimental.pallas import tpu as pltpu
from jax.sharding import Mesh
from jax.sharding import PartitionSpec as P

EPS = 1e-06
PIECE = 256
LANES = 128
HIGH, LOW = 64, 32
SUMS = 3
FIRST_Y = (7, 4)
FIRST_Z = (4, 7)


def project(pooled, weights, copies, core_ref, keep_ref, send_ref):
    total = None
    for copy, first, last in copies:
        copy.wait()
        piece = jnp.dot(
            pooled[:, first:last], weights[first:last, :], preferred_element_type=jnp.float32
        )
        total = piece if total is None else total + piece
    share = keep_ref.shape[0]
    upper, lower = total[:share], total[share:]
    first_core = core_ref[0] == 0
    keep_ref[...] = jnp.where(first_core, upper, lower)
    send_ref[...] = jnp.where(first_core, lower, upper)


def fetch(slices_hbm, weights_hbm, slices, weights, sems):
    depth = weights_hbm.shape[0]
    first_copy = pltpu.make_async_copy(slices_hbm, slices, sems.at[0])
    first_copy.start()
    copies = []
    for place, first in enumerate(range(0, depth, PIECE)):
        last = min(first + PIECE, depth)
        copy = pltpu.make_async_copy(
            weights_hbm.at[first:last], weights.at[first:last], sems.at[1 + place]
        )
        copy.start()
        copies.append((copy, first, min(first + PIECE, weights.shape[0])))
    return first_copy, copies


def image_kernel(core_ref, slices_hbm, weights_hbm, keep_ref, send_ref, slices, weights, sems):
    first_copy, copies = fetch(slices_hbm, weights_hbm, slices, weights, sems)
    width = weights_hbm.shape[0]
    patch_count = slices.shape[1] // width
    first_copy.wait()
    summed = slices[:, :width].astype(jnp.float32)
    for patch in range(1, patch_count):
        summed += slices[:, patch * width : (patch + 1) * width].astype(jnp.float32)
    pooled = (summed / patch_count).astype(jnp.bfloat16)
    project(pooled, weights, copies, core_ref, keep_ref, send_ref)


def text_kernel(
    core_ref, lengths_hbm, slices_hbm, weights_hbm, keep_ref, send_ref, slices, weights, sems, lengths_ref
):
    lengths_copy = pltpu.make_async_copy(lengths_hbm, lengths_ref, sems.at[sems.shape[0] - 1])
    lengths_copy.start()
    first_copy, copies = fetch(slices_hbm, weights_hbm, slices, weights, sems)
    width = weights_hbm.shape[0]
    row_count = slices.shape[0]
    slot_count = slices.shape[1] // width
    padded = weights.shape[0]
    if padded > width:
        weights[width:, :] = jnp.zeros((padded - width, weights.shape[1]), jnp.bfloat16)
    shape = (row_count, 2 * width)
    row = lax.broadcasted_iota(jnp.int32, shape, 0)
    lengths = jnp.zeros(shape, jnp.int32)
    lengths_copy.wait()
    for index in range(row_count):
        lengths = jnp.where(row == index, lengths_ref[index], lengths)
    second = (lax.broadcasted_iota(jnp.int32, shape, 1) >= width).astype(jnp.int32)
    left = lengths - second
    first_copy.wait()
    summed = jnp.zeros(shape, jnp.float32)
    for slot in range(0, slot_count, 2):
        piece = slices[:, slot * width : (slot + 2) * width].astype(jnp.float32)
        summed += jnp.where(slot < left, piece, 0.0)
    summed = summed + pltpu.roll(summed, width, 1)
    pooled = (summed / lengths.astype(jnp.float32)).astype(jnp.bfloat16)
    project(pooled, weights, copies, core_ref, keep_ref, send_ref)


def pooled_partial(kernel, core_index, slices, weights, lengths=None):
    row_count = slices.shape[0]
    depth, width = weights.shape
    padded = -(-depth // LANES) * LANES
    pieces = -(-depth // PIECE)
    any_space = pl.BlockSpec(memory_space=pl.ANY)
    half = jax.ShapeDtypeStruct((row_count // 2, width), jnp.float32)
    given = (slices, weights) if lengths is None else (lengths, slices, weights)
    scratch = [
        pltpu.VMEM(slices.shape, jnp.bfloat16),
        pltpu.VMEM((padded, width), jnp.bfloat16),
        pltpu.SemaphoreType.DMA((2 + pieces,)),
    ]
    if lengths is not None:
        scratch.append(pltpu.SMEM(lengths.shape, jnp.int32))
    return pl.pallas_call(
        kernel,
        out_shape=(half, half),
        in_specs=[pl.BlockSpec(memory_space=pltpu.SMEM)] + [any_space] * len(given),
        out_specs=(pl.BlockSpec(memory_space=pltpu.VMEM),) * 2,
        scratch_shapes=scratch,
        compiler_params=pltpu.CompilerParams(vmem_limit_bytes=32 * 2**20),
    )(core_index, *given)


def staggered(blocks, axis, firsts):
    members = lax.axis_size(axis)
    cores = lax.axis_size("mp")
    groups = [
        [(at + firsts[core]) % members * cores + core for at in range(members)]
        for core in range(cores)
    ]
    return lax.all_to_all(blocks, (axis, "mp"), 0, 0, axis_index_groups=groups, tiled=True)


def swap_gather(block, axis):
    members = lax.axis_size(axis)
    half = members // 2

    def brought(value, across):
        return lax.ppermute(value, axis, [(index, index ^ across) for index in range(members)])

    pair = jnp.concatenate([block, brought(block, half)], axis=0)
    wide = pair.astype(jnp.float32)
    passed = jnp.sum(wide, axis=0, keepdims=True)
    for _ in range(SUMS - 1):
        passed = jnp.sum(wide * passed, axis=0, keepdims=True)
    pair = pair + (passed * 0).astype(pair.dtype)
    return jnp.concatenate([pair] + [brought(pair, across) for across in range(1, half)], axis=0)


def in_order(held, axis, size, firsts, last):
    members = lax.axis_size(axis)
    place = lax.broadcasted_iota(jnp.int32, (members * size, members * size), 0)
    slot = lax.broadcasted_iota(jnp.int32, (members * size, members * size), 1)
    number = slot // size
    came_from = lax.axis_index(axis) ^ (number // 2 + (number % 2) * (members // 2))
    first = jnp.where(lax.axis_index("mp") == 0, firsts[0], firsts[1])
    member = (place // size + first) % members
    moves = (member == came_from) & (place % size == slot % size)
    moves = moves.astype(held.dtype) + last[: members * size, : members * size] * 0
    ordered = jnp.dot(moves, held, preferred_element_type=jnp.float32)
    return ordered.astype(held.dtype)


def final_kernel(scale_ref, total_ref, embedding_ref, grads_hbm, losses_hbm, grads, losses, sems):
    share, width = embedding_ref.shape
    loss = total_ref[:, width : width + 1] + total_ref[:, width + 1 : width + 2]
    row = lax.broadcasted_iota(jnp.int32, (share, LANES), 0)
    column = lax.broadcasted_iota(jnp.int32, (share, LANES), 1)
    diagonal = jnp.where(row == column, jnp.broadcast_to(loss, (share, LANES)), 0.0)
    losses[...] = jnp.sum(diagonal, axis=0, keepdims=True)[:, :share]
    losses_copy = pltpu.make_async_copy(losses, losses_hbm, sems.at[0])
    losses_copy.start()
    embedding = embedding_ref[...]
    inverse = lax.rsqrt(jnp.sum(embedding * embedding, axis=1, keepdims=True) + EPS)
    unit = embedding * inverse
    grad_sum = jnp.exp(jnp.full((1, LANES), scale_ref[0], jnp.float32))[:, :1] * total_ref[:, :width]
    along = jnp.sum(unit * grad_sum, axis=1, keepdims=True)
    grads[0] = inverse * (grad_sum - unit * along)
    grads_copy = pltpu.make_async_copy(grads, grads_hbm, sems.at[1])
    grads_copy.start()
    losses_copy.wait()
    grads_copy.wait()


def shards(tower_inputs, image_proj, text_proj, text_lengths, partner, log_scale, bias):
    slices = tower_inputs[0, :, 0, :]
    row_count = slices.shape[0]
    tower = lax.axis_index("tower")
    core = lax.axis_index("mp")
    n_mp = lax.axis_size("mp")
    n_y = lax.axis_size("y")
    n_x = lax.axis_size("x")
    n_z = lax.axis_size("z")
    share = row_count // n_mp
    width = image_proj.shape[1]

    def pair_at(z_at, x_at, y_at):
        return ((z_at * n_x + x_at) * n_y + y_at) * row_count

    core_index = core.astype(jnp.int32).reshape(1)
    kept, sent = lax.cond(
        tower == 0,
        lambda: pooled_partial(image_kernel, core_index, slices, image_proj),
        lambda: pooled_partial(text_kernel, core_index, slices, text_proj, text_lengths),
    )
    embedding = kept + lax.ppermute(sent, "mp", [(0, 1), (1, 0)])
    inverse = lax.rsqrt(jnp.sum(embedding * embedding, axis=1, keepdims=True) + EPS)
    unit = embedding * inverse
    unit_low = unit.astype(jnp.bfloat16)

    first = pair_at(lax.axis_index("z"), lax.axis_index("x"), lax.axis_index("y")) + core * share
    partners = lax.dynamic_slice_in_dim(partner, core * share, share, 0)
    key = jnp.where(tower == 0, partners, first + lax.iota(jnp.int32, share))[:, None]
    column = lax.broadcasted_iota(jnp.int32, (share, LANES), 1)
    coded = (column == key // LOW) | (column == HIGH + key % LOW)
    key_block = coded.astype(jnp.bfloat16)
    own = jnp.concatenate([unit_low, key_block], axis=1)

    near = lax.ppermute(own, "tower", [(0, 1), (1, 0)])
    across = lax.ppermute(own, ("tower", "x"), [(0, 3), (3, 0), (1, 2), (2, 1)])
    temper = jnp.exp(log_scale[0])
    other = jnp.concatenate([near, across], axis=0) + (temper * 0).astype(near.dtype)
    copies = jnp.broadcast_to(other[None], (n_y,) + other.shape)
    held = swap_gather(own, "z")
    other_mine = staggered(copies, "y", FIRST_Y)
    other_mine = other_mine.reshape(n_y * n_x * share, width + LANES)
    other_theirs = lax.ppermute(other_mine, "mp", [(0, 1), (1, 0)])
    own_all = in_order(held, "z", share, FIRST_Z, other_mine)

    own_low = own_all[:, :width]

    def products(rows, columns):
        return lax.dot_general(
            rows, columns, (((1,), (1,)), ((), ())), preferred_element_type=jnp.float32
        )

    def score(others):
        other_low = others[:, :width]
        logits = temper * products(own_low, other_low) + bias[0]
        paired = products(own_all[:, width:], others[:, width:]) > 1.5
        losses = jax.nn.softplus(jnp.where(paired, -logits, logits))
        weights = (jax.nn.sigmoid(logits) - paired.astype(jnp.float32)).astype(jnp.bfloat16)
        grad = jnp.dot(weights, other_low, preferred_element_type=jnp.float32)
        return grad, jnp.sum(losses, axis=1, keepdims=True)

    grad_mine, loss_mine = score(other_mine)
    grad_theirs, loss_theirs = score(other_theirs)
    grad_part = grad_mine + grad_theirs
    loss_part = loss_mine + loss_theirs

    loss_high = lax.reduce_precision(loss_part, 5, 10)
    loss_rest = loss_part - loss_high
    lane = lax.broadcasted_iota(jnp.int32, (n_z * share, LANES), 1)
    loss_block = jnp.where(lane == 0, loss_high, loss_rest).astype(jnp.float16)
    sums = jnp.concatenate([grad_part.astype(jnp.float16), loss_block], axis=1)
    sums = staggered(sums.reshape(n_z, share, width + LANES), "z", FIRST_Z)
    total = jnp.sum(sums.astype(jnp.float32), axis=0)
    vmem = pl.BlockSpec(memory_space=pltpu.VMEM)
    any_space = pl.BlockSpec(memory_space=pl.ANY)
    return pl.pallas_call(
        final_kernel,
        out_shape=(
            jax.ShapeDtypeStruct((1, share, width), jnp.float32),
            jax.ShapeDtypeStruct((1, share), jnp.float32),
        ),
        in_specs=[pl.BlockSpec(memory_space=pltpu.SMEM), vmem, vmem],
        out_specs=(any_space, any_space),
        scratch_shapes=[
            pltpu.VMEM((1, share, width), jnp.float32),
            pltpu.VMEM((1, share), jnp.float32),
            pltpu.SemaphoreType.DMA((2,)),
        ],
        compiler_params=pltpu.CompilerParams(vmem_limit_bytes=8 * 2**20),
    )(log_scale, total, embedding)


def solution(mesh):
    n_tower, n_blk, n_mp = (mesh.shape[name] for name in ("tower", "blk", "mp"))
    n_z, n_x = 8, 2
    grid = Mesh(
        mesh.devices.reshape(n_tower, n_z, n_x, n_blk // (n_z * n_x), n_mp),
        ("tower", "z", "x", "y", "mp"),
    )
    blk = ("z", "x", "y")
    placed = (
        P("tower", blk, "mp", None),
        P("mp", None),
        P("mp", None),
        P(blk),
        P(blk),
        P(),
        P(),
    )
    return jax.shard_map(
        shards,
        mesh=grid,
        in_specs=placed,
        out_specs=(P("tower", blk + ("mp",), None), P("tower", blk + ("mp",))),
        check_vma=False,
    )
```
